512 devices in a mesh: dp: 2 (over z_hi), ctx: 32 (over y, z_lo), tensor: 8 (over x, core).
Axes of the slice: x: 4, y: 8, z: 8 (z_hi: 2, z_lo: 4; z = z_hi * 4 + z_lo), core: 2. Of those that a mesh axis runs over, the one named last changes fastest.
Arguments:
- left_gate: bfloat16 [2, 4096, 4096], P('dp', 'ctx', 'tensor'), may hold values from -6 to 6
- right_gate: bfloat16 [2, 4096, 4096], P('dp', 'ctx', 'tensor'), may hold values from -6 to 6
- values: bfloat16 [2, 4096, 4096], P('dp', 'ctx', 'tensor'), may hold values from -6 to 6
- grad_out: bfloat16 [2, 4096, 4096], P('dp', 'ctx', 'tensor'), may hold values from -6 to 6
- residues: float32 [256, 16], replicated, may hold values from -0.09375 to 0.09375
- decay_rates: float32 [256, 16], replicated, may hold values from 0.5 to 128
Outputs:
- gated_out: bfloat16 [2, 4096, 4096], P('dp', 'ctx', 'tensor')
- grad_left: bfloat16 [2, 4096, 4096], P('dp', 'ctx', 'tensor')
- grad_right: bfloat16 [2, 4096, 4096], P('dp', 'ctx', 'tensor')
- grad_values: bfloat16 [2, 4096, 4096], P('dp', 'ctx', 'tensor')
- grad_residues: float32 [256, 16], replicated
- grad_rates: float32 [256, 16], replicated
The draws below stay inside these ranges and needn't reach their ends.
All inputs are finite; a program needn't handle non-finite values.
Results may differ from the reference program's by a relative error of at most 0.0065.
Values may be sent and summed in bfloat16 or wider, within the bound.
A program may use at most 64 MiB of HBM per device.

```python
import math
import jax
import jax.numpy as jnp
from jax import lax

CH = 4096
GSIZE = 16
ORD = 16
GROUPS = 256
SEQ = 4096
N_DP = 2


def levels(own_key, extent, pieces, smallest, largest):
    def one(axis_at, shards_of):
        steps = jax.random.uniform(jax.random.fold_in(jax.random.fold_in(own_key, 6), axis_at), (shards_of,), jnp.float32, smallest / len(pieces), largest / len(pieces))
        return jnp.repeat(jnp.exp(steps), extent[axis_at] // shards_of).reshape((-1,) + (1,) * (len(extent) - axis_at - 1))

    level = one(*pieces[0])
    for cut in pieces[1:]:
        level = level * one(*cut)
    return level


def bell_draw(key, extent, deviation, reach, cuts=(), held_as=jnp.bfloat16):
    values = deviation * jax.random.normal(key, extent, jnp.float32)
    if cuts:
        values = values * levels(key, extent, cuts, -0.22, 0.18)
    return jnp.clip(values, -reach, reach).astype(held_as)


def setup_inputs(seed: int = 0) -> dict:
    seeds = jax.random.split(jax.random.key(seed), 7)
    left_gate = bell_draw(seeds[0], (N_DP, SEQ, CH), 1.0, 6.0, ((0, 2), (1, 32), (2, 8)))
    right_gate = bell_draw(seeds[1], (N_DP, SEQ, CH), 1.0, 6.0, ((0, 2), (1, 32), (2, 8)))
    values = bell_draw(seeds[2], (N_DP, SEQ, CH), 1.0, 6.0, ((0, 2), (1, 32), (2, 8)))
    grad_out = bell_draw(seeds[3], (N_DP, SEQ, CH), 1.0, 6.0, ((0, 2), (1, 32), (2, 8)))
    residues = bell_draw(seeds[4], (GROUPS, ORD), (1.0 / SEQ ** 0.5), 0.09375, (), jnp.float32)
    decay_rates = jnp.clip(jnp.exp(jax.random.uniform(seeds[5], (GROUPS, ORD), jnp.float32, math.log(0.5), math.log(128.0))), 0.5, 128.0)
    return dict(left_gate=left_gate, right_gate=right_gate, values=values, grad_out=grad_out, residues=residues, decay_rates=decay_rates)


clip_bound = 32.0

def rounded(array):
    return lax.optimization_barrier(array.astype(jnp.bfloat16)).astype(jnp.float32)

def reference(left_gate, right_gate, values, grad_out, residues, decay_rates):
    block_channels = 128
    block_groups = block_channels // GSIZE
    total_len = 2 * SEQ
    offsets = jnp.arange(SEQ).astype(jnp.float32)

    def one_block(index):
        start = index * block_channels

        def window(array):
            return lax.dynamic_slice_in_dim(array, start, block_channels, 2).astype(jnp.float32)
        left_part = window(left_gate)
        right_part = window(right_gate)
        value_part = window(values)
        grad_part = window(grad_out)
        res_part = lax.dynamic_slice_in_dim(residues, index * block_groups, block_groups, 0)
        rate_part = lax.dynamic_slice_in_dim(decay_rates, index * block_groups, block_groups, 0)
        decay_table = jnp.exp(-(rate_part[None, :, :] * offsets[:, None, None]) / SEQ)
        filters = rounded(lax.optimization_barrier(jnp.sum(res_part[None, :, :] * decay_table, axis=2)))
        per_channel = jnp.repeat(filters, GSIZE, axis=1)
        gated_in = rounded(left_part * value_part)
        signal = rounded(right_part * grad_part)
        gated_spec = jnp.fft.rfft(gated_in, n=total_len, axis=1)
        signal_spec = jnp.fft.rfft(signal, n=total_len, axis=1)
        filter_spec = jnp.fft.rfft(per_channel, n=total_len, axis=0)[None]
        conv_out = rounded(jnp.fft.irfft(gated_spec * filter_spec, n=total_len, axis=1)[:, :SEQ])
        conv_grad = rounded(jnp.fft.irfft(signal_spec * jnp.conj(filter_spec), n=total_len, axis=1)[:, :SEQ])
        cross = (signal_spec * jnp.conj(gated_spec)).reshape(N_DP, SEQ + 1, block_groups, GSIZE).sum(axis=3)
        filter_grad = rounded(jnp.fft.irfft(cross, n=total_len, axis=1)[:, :SEQ])
        mixed_out = (right_part * conv_out).astype(jnp.bfloat16)
        grad_right = (grad_part * conv_out).astype(jnp.bfloat16)
        grad_left = (conv_grad * value_part).astype(jnp.bfloat16)
        grad_vals = (conv_grad * left_part).astype(jnp.bfloat16)
        grad_res = jnp.einsum('btg,tgn->gn', filter_grad, decay_table, precision=lax.Precision.HIGHEST)
        weighted = decay_table * (-offsets / SEQ)[:, None, None]
        grad_rate = jnp.einsum('btg,tgn->gn', filter_grad, weighted, precision=lax.Precision.HIGHEST) * res_part
        return (mixed_out, grad_left, grad_right, grad_vals, grad_res, grad_rate)
    results = lax.map(one_block, jnp.arange(CH // block_channels, dtype=jnp.int32))

    def joined(stack):
        return jnp.moveaxis(stack, 0, 2).reshape(N_DP, SEQ, CH)
    raw_res = results[4].reshape(GROUPS, ORD)
    raw_rates = results[5].reshape(GROUPS, ORD)
    grad_norm = jnp.sqrt(jnp.sum(raw_res * raw_res) + jnp.sum(raw_rates * raw_rates))
    factor = clip_bound / jnp.maximum(grad_norm, clip_bound)
    return (joined(results[0]), joined(results[1]), joined(results[2]), joined(results[3]), raw_res * factor, raw_rates * factor)
```

```python
import functools

import jax
import jax.numpy as jnp
from jax import lax
from jax.experimental import pallas as pl
from jax.experimental.pallas import tpu as pltpu
from jax.sharding import PartitionSpec as P

MESH = pl.DeviceIdType.MESH
BF = jnp.bfloat16
F32 = jnp.float32
GSIZE = 16
ORD = 16
TILE = 128
PER_TILE = TILE // GSIZE
CLIP = 32.0
NT = (((1,), (1,)), ((), ()))
NN = (((1,), (0,)), ((), ()))


def dot(a, b, dims=NN):
    return lax.dot_general(a, b, dims, preferred_element_type=F32)


def split(x):
    hi = x.astype(BF)
    return hi, (x - hi.astype(F32)).astype(BF)


def lanes8(x):
    return jnp.concatenate([x] * PER_TILE, axis=1)


def shift(x, amount):
    amount = amount % TILE
    return x if amount == 0 else pltpu.roll(x, amount, 1)


def decays(rate, positions, top=None):
    sub = lax.broadcasted_iota(jnp.int32, (8, TILE), 0).astype(F32)
    blocks = positions // 8
    step = jnp.exp(-8.0 * rate)
    now = jnp.exp(-rate * (sub if top is None else top - (positions - 8) - sub))
    rows = [now]
    for _ in range(blocks - 1):
        now = now * step
        rows.append(now)
    if top is not None:
        rows = rows[::-1]
    return jnp.concatenate(rows, axis=0)


def kernel(
    n_ctx,
    n_tensor,
    n_dp,
    left_hbm,
    right_hbm,
    values_hbm,
    grad_hbm,
    res_hbm,
    rate_hbm,
    out_conv,
    out_left,
    out_right,
    out_values,
    out_res,
    out_rate,
    vin,
    par,
    gst,
    tables,
    taps,
    convs,
    msg1,
    recv1,
    lag1,
    lagr,
    msg2,
    recv2,
    msg3,
    recv3,
    vout,
    gout,
    in_sem,
    par_sem,
    send_sem,
    recv_sem,
    out_sem,
):
    me = lax.axis_index("ctx")
    my_t = lax.axis_index("tensor")
    my_d = lax.axis_index("dp")
    positions = vin.shape[2]
    tiles = vin.shape[1]
    seq = n_ctx * positions
    groups = tiles * PER_TILE
    n_side = n_dp * n_tensor
    my_side = my_d * n_tensor + my_t
    inv = 1.0 / seq

    barrier = pltpu.get_barrier_semaphore()

    def greet_ctx(o, carry):
        peer = lax.rem(me + o, n_ctx)
        pl.semaphore_signal(barrier, inc=1, device_id={"ctx": peer}, device_id_type=MESH)
        return carry

    lax.fori_loop(1, n_ctx, greet_ctx, 0)

    def greet_side(o, carry):
        peer = lax.rem(my_side + o, n_side)
        pl.semaphore_signal(
            barrier,
            inc=1,
            device_id={"dp": peer // n_tensor, "tensor": lax.rem(peer, n_tensor)},
            device_id_type=MESH,
        )
        return carry

    lax.fori_loop(1, n_side, greet_side, 0)

    for k, ref in enumerate((res_hbm, rate_hbm)):
        pltpu.make_async_copy(ref, gout.at[k], par_sem).start()
    for j in range(tiles):
        for a, ref in enumerate((left_hbm, values_hbm, right_hbm, grad_hbm)):
            pltpu.make_async_copy(
                ref.at[:, pl.ds(j * TILE, TILE)], vin.at[a, j], in_sem.at[j]
            ).start()
    pltpu.make_async_copy(gout, gout, par_sem).wait()
    for k in range(2):
        par[k] = gout[k].T
    first = pl.multiple_of(my_t * groups, groups)

    lane = lax.broadcasted_iota(jnp.int32, (8, TILE), 1)
    sub = lax.broadcasted_iota(jnp.int32, (8, TILE), 0)
    block = lane // GSIZE
    row_i = lax.broadcasted_iota(jnp.int32, (TILE, TILE), 0)
    col_i = lax.broadcasted_iota(jnp.int32, (TILE, TILE), 1)
    pos_col = row_i.astype(F32)

    pl.semaphore_wait(barrier, n_ctx - 1 + n_side - 1)

    def states(j, carry):
        pick = pl.ds(pl.multiple_of(first + j * PER_TILE, PER_TILE), PER_TILE)
        rates = jnp.where(block == sub, lanes8(par[1, pick, :]), 0.0)
        resid = jnp.where(block == sub, lanes8(par[0, pick, :]), 0.0)
        rate = jnp.sum(rates, axis=0, keepdims=True) * inv
        ahead = decays(rate, positions, positions)
        ahead1 = decays(shift(rate, 16), positions, positions) * (positions - pos_col)
        after2 = decays(shift(rate, 32), positions) * pos_col
        after = decays(shift(rate, 48), positions)
        q_hi, q_lo = split(ahead)
        p_hi, p_lo = split(after)
        tables[j, 0] = q_hi
        tables[j, 1] = q_lo
        tables[j, 2] = p_hi
        tables[j, 3] = p_lo
        r_hi, r_lo = split(shift(resid, 48))
        taps[j] = dot(r_hi, p_hi, NT) + (dot(r_lo, p_hi, NT) + dot(r_hi, p_lo, NT))

        pltpu.make_async_copy(vin.at[:, j], vin.at[:, j], in_sem.at[j]).wait()
        gated = (vin[0, j].astype(F32) * vin[1, j].astype(F32)).astype(BF)
        signal = (vin[2, j].astype(F32) * vin[3, j].astype(F32)).astype(BF)
        gst[0, j] = gated
        gst[1, j] = signal
        gated_t = gated.T
        signal_t = signal.T
        gst[2, j] = gated_t
        gst[3, j] = signal_t
        kinds = (
            dot(gated_t, q_hi) + dot(gated_t, q_lo),
            dot(gated_t, ahead1.astype(BF)),
            dot(signal_t, after2.astype(BF)),
            dot(signal_t, p_hi) + dot(signal_t, p_lo),
        )
        for g in range(PER_TILE):
            which = (block - g) & 7
            halves = []
            for half in range(2):
                at = g * GSIZE + 8 * half
                part = kinds[3][at : at + 8]
                for k in (2, 1, 0):
                    part = jnp.where(which == k, kinds[k][at : at + 8], part)
                halves.append(part)
            msg1[j * PER_TILE + g] = jnp.where(which < 4, halves[0], shift(halves[1], 64))
        return carry

    lax.fori_loop(0, tiles, states, 0)

    def exchange(src, dst, k):
        def one(o, carry):
            peer = lax.rem(me + o, n_ctx)
            pltpu.make_async_remote_copy(
                src_ref=src.at[peer],
                dst_ref=dst.at[me],
                send_sem=send_sem.at[k],
                recv_sem=recv_sem.at[k],
                device_id={"ctx": peer},
                device_id_type=MESH,
            ).start()
            return carry

        lax.fori_loop(1, n_ctx, one, 0)
        dst[me] = src[me]

    def landed(dst, k, count):
        part = dst.at[pl.ds(0, count)]
        pltpu.make_async_copy(part, part, recv_sem.at[k]).wait()

    def sent(src, k, count):
        part = src.at[pl.ds(0, count)]
        pltpu.make_async_copy(part, part, send_sem.at[k]).wait()

    exchange(msg1, recv1, 0)

    later = col_i >= row_i
    mirror = row_i + col_i
    flip = jnp.where(mirror == positions - 1, 1.0, 0.0).astype(BF)

    def lags(j, carry):
        gated = gst[0, j]
        signal = dot(flip, gst[1, j]).astype(BF)
        for g in range(PER_TILE):
            only = jnp.where(col_i // GSIZE == g, gated.astype(F32), 0.0).astype(BF)
            pair = jnp.where(mirror < positions, dot(only, signal, NT), 0.0)
            skew = pltpu.roll(pair, 0, 1, stride=1, stride_axis=0)
            lag1[j * PER_TILE + g] = jnp.sum(skew, axis=0, keepdims=True)
        return carry

    lax.fori_loop(0, tiles, lags, 0)
    exchange(lag1, lagr, 1)

    def inside(j, carry):
        rows = taps[j].astype(BF).astype(F32)
        for g in range(PER_TILE):
            wide = jnp.broadcast_to(rows[g : g + 1], (TILE, TILE))
            turned = pltpu.roll(wide, 0, 1, stride=1, stride_axis=0)
            upper = jnp.where(later, turned, 0.0).astype(BF)
            at = g * GSIZE
            convs[0, j, at : at + GSIZE, :] = dot(gst[2, j, at : at + GSIZE, :], upper)
            convs[1, j, at : at + GSIZE, :] = dot(gst[3, j, at : at + GSIZE, :], upper, NT)
        return carry

    lax.fori_loop(0, tiles, inside, 0)

    rate_d = lanes8(par[1, pl.ds(first + me, 1), :]) * inv
    res_d = lanes8(par[0, pl.ds(first + me, 1), :])
    decay_d = decays(rate_d, positions, positions - 1)
    dec = jnp.exp(-rate_d * positions)
    kind = (block - me) & 3
    is0, is1, is2, is3 = [kind == k for k in range(4)]

    landed(recv1, 0, n_ctx - 1)
    back = jnp.zeros((8, TILE), F32)
    for i in reversed(range(n_ctx)):
        msg2[i] = back
        back = back * dec + recv1[i]
    front = jnp.zeros((8, TILE), F32)
    sum_r = jnp.zeros((8, TILE), F32)
    sum_s = jnp.zeros((8, TILE), F32)
    sum_m = jnp.zeros((8, TILE), F32)
    for i in range(n_ctx):
        own = recv1[i]
        behind = msg2[i]
        behind0 = shift(behind, 80)
        own0 = shift(own, 80)
        mixed = shift(jnp.where(is2, own, behind), 96)
        sum_r = sum_r + front * own0
        sum_m = sum_m + front * behind0
        sum_s = sum_s + jnp.where(is0, front, own) * mixed
        msg2[i] = jnp.where(is0, behind0, shift(front, 48)) * res_d
        front = front * dec + own

    def fold(x):
        x = jnp.sum(x, axis=0, keepdims=True)
        return x + shift(x, 64)

    raw_r = fold(sum_r)
    raw_s = fold(jnp.where(is0, sum_s + (positions * dec) * sum_m, 0.0)) + shift(
        fold(jnp.where(is1, sum_s, 0.0)), 112
    )
    landed(lagr, 1, n_ctx - 1)
    lag = jnp.sum(lagr[...], axis=0)
    weighted = jnp.where(sub == 0, lag, jnp.where(sub == 1, lag * (positions - 1 - lane).astype(F32), 0.0))
    close = lax.dot_general(
        weighted, decay_d, NN, precision=lax.Precision.HIGHEST, preferred_element_type=F32
    )
    raw_r = shift(raw_r + close[0:1], 16)
    raw_s = shift((raw_s + close[1:2]) * res_d * (-inv), 32)
    grads = jnp.where(is1, raw_r, raw_s)
    keep = is0 | is3
    for i in range(n_ctx):
        msg2[i] = jnp.where(keep, msg2[i], grads)
    exchange(msg2, recv2, 2)
    landed(recv2, 2, n_ctx - 1)

    pack = jnp.zeros((8, TILE), F32)
    for g in range(groups):
        row, quarter = g % 8, g // 8
        moved = shift(recv2[g], 16 * (2 * quarter - row - 1))
        pack = jnp.where((sub == row) & (block // 2 == quarter), moved, pack)
    msg3[...] = pack

    def side(o, carry):
        peer = lax.rem(my_side + o, n_side)
        pltpu.make_async_remote_copy(
            src_ref=msg3,
            dst_ref=recv3.at[my_side],
            send_sem=send_sem.at[3],
            recv_sem=recv_sem.at[3],
            device_id={"dp": peer // n_tensor, "tensor": lax.rem(peer, n_tensor)},
            device_id_type=MESH,
        ).start()
        return carry

    lax.fori_loop(1, n_side, side, 0)
    recv3[my_side] = pack

    outs = (out_conv, out_left, out_right, out_values)

    def finish(j, carry):
        heads = []
        tails = []
        for g in range(PER_TILE):
            m = recv2[j * PER_TILE + g]
            turned = shift(m, 64)
            for part in (m, turned):
                tails.append(jnp.where(block == g, part, 0.0))
                heads.append(jnp.where(block == (g + 3) % 8, part, 0.0))
        h_hi, h_lo = split(jnp.concatenate(heads, axis=0))
        b_hi, b_lo = split(jnp.concatenate(tails, axis=0))
        q_hi, q_lo, p_hi, p_lo = [tables[j, k] for k in range(4)]
        conv = convs[0, j] + (
            dot(h_hi, p_hi, NT) + (dot(h_lo, p_hi, NT) + dot(h_hi, p_lo, NT))
        )
        conv_grad = convs[1, j] + (
            dot(b_hi, q_hi, NT) + (dot(b_lo, q_hi, NT) + dot(b_hi, q_lo, NT))
        )
        conv = conv.astype(BF).T.astype(F32)
        conv_grad = conv_grad.astype(BF).T.astype(F32)
        vout[0, j] = (vin[2, j].astype(F32) * conv).astype(BF)
        vout[1, j] = (conv_grad * vin[1, j].astype(F32)).astype(BF)
        vout[2, j] = (vin[3, j].astype(F32) * conv).astype(BF)
        vout[3, j] = (conv_grad * vin[0, j].astype(F32)).astype(BF)
        columns = pl.ds(pl.multiple_of(j * TILE, TILE), TILE)
        for a, ref in enumerate(outs):
            pltpu.make_async_copy(vout.at[a, j], ref.at[:, columns], out_sem.at[0]).start()
        return carry

    lax.fori_loop(0, tiles, finish, 0)

    landed(recv3, 3, n_side - 1)
    total = jnp.zeros((8, TILE), F32)
    summed = []
    for t in range(n_tensor):
        both = recv3[t]
        for d in range(1, n_dp):
            both = both + recv3[d * n_tensor + t]
        summed.append(both)
        total = total + both * both
    total = jnp.sum(jnp.sum(total, axis=0, keepdims=True), axis=1, keepdims=True)
    factor = CLIP / jnp.maximum(jnp.sqrt(total), CLIP)
    width = TILE // groups
    for at in range(0, n_tensor, width):
        rows = []
        for t in range(at, at + width):
            scaled = summed[t] * factor
            rows += [shift(scaled, -32 * quarter) for quarter in range(tiles)]
        turned = jnp.concatenate(rows, axis=0).T
        columns = slice(at * groups, (at + width) * groups)
        for k in range(2):
            gout[k, :, columns] = turned[k * ORD : (k + 1) * ORD]
    pltpu.make_async_copy(gout.at[0], out_res, out_sem.at[1]).start()
    pltpu.make_async_copy(gout.at[1], out_rate, out_sem.at[1]).start()

    sent(msg1, 0, n_ctx - 1)
    sent(lag1, 1, n_ctx - 1)
    sent(msg2, 2, n_ctx - 1)
    sent(recv3, 3, n_side - 1)
    pltpu.make_async_copy(vout, vout, out_sem.at[0]).wait()
    pltpu.make_async_copy(gout, gout, out_sem.at[1]).wait()


def solution(mesh):
    n_ctx, n_tensor, n_dp = mesh.shape["ctx"], mesh.shape["tensor"], mesh.shape["dp"]
    n_side = n_tensor * n_dp

    def on_device(left_gate, right_gate, values, grad_out, residues, decay_rates):
        positions, channels = left_gate.shape[1:]
        tiles = channels // TILE
        groups = channels // GSIZE
        flat = [x.reshape(positions, channels) for x in (left_gate, right_gate, values, grad_out)]
        wide = jax.ShapeDtypeStruct((positions, channels), BF)
        small = jax.ShapeDtypeStruct(residues.shape[::-1], F32)
        anywhere = pl.BlockSpec(memory_space=pl.ANY)
        outs = pl.pallas_call(
            functools.partial(kernel, n_ctx, n_tensor, n_dp),
            out_shape=(wide, wide, wide, wide, small, small),
            in_specs=[anywhere] * 6,
            out_specs=(anywhere,) * 6,
            scratch_shapes=[
                pltpu.VMEM((4, tiles, positions, TILE), BF),
                pltpu.VMEM((2,) + residues.shape, F32),
                pltpu.VMEM((4, tiles, TILE, TILE), BF),
                pltpu.VMEM((tiles, 4, positions, TILE), BF),
                pltpu.VMEM((tiles, PER_TILE, positions), F32),
                pltpu.VMEM((2, tiles, TILE, positions), F32),
                pltpu.VMEM((n_ctx, 8, TILE), F32),
                pltpu.VMEM((n_ctx, 8, TILE), F32),
                pltpu.VMEM((n_ctx, 1, TILE), F32),
                pltpu.VMEM((n_ctx, 1, TILE), F32),
                pltpu.VMEM((n_ctx, 8, TILE), F32),
                pltpu.VMEM((n_ctx, 8, TILE), F32),
                pltpu.VMEM((8, TILE), F32),
                pltpu.VMEM((n_side, 8, TILE), F32),
                pltpu.VMEM((4, tiles, positions, TILE), BF),
                pltpu.VMEM((2,) + residues.shape[::-1], F32),
                pltpu.SemaphoreType.DMA((tiles,)),
                pltpu.SemaphoreType.DMA,
                pltpu.SemaphoreType.DMA((4,)),
                pltpu.SemaphoreType.DMA((4,)),
                pltpu.SemaphoreType.DMA((2,)),
            ],
            compiler_params=pltpu.CompilerParams(
                collective_id=0, has_side_effects=True, vmem_limit_bytes=16 * 1024 * 1024
            ),
        )(*flat, residues.T, decay_rates.T)
        full = [x.reshape(1, positions, channels) for x in outs[:4]]
        return (*full, outs[4].T, outs[5].T)

    wide = P("dp", "ctx", "tensor")
    return jax.shard_map(
        on_device,
        mesh=mesh,
        in_specs=(wide, wide, wide, wide, P(), P()),
        out_specs=(wide, wide, wide, wide, P(), P()),
        check_vma=False,
    )
```

```python
import functools

import jax
import jax.numpy as jnp
from jax import lax
from jax.experimental import pallas as pl
from jax.experimental.pallas import tpu as pltpu
from jax.sharding import PartitionSpec as P

MESH = pl.DeviceIdType.MESH
BF = jnp.bfloat16
F32 = jnp.float32
GSIZE = 16
ORD = 16
TILE = 128
PER_TILE = TILE // GSIZE
CLIP = 32.0
N_Z = 4
N_CORE = 2
NT = (((1,), (1,)), ((), ()))
NN = (((1,), (0,)), ((), ()))


def dot(a, b, dims=NN):
    return lax.dot_general(a, b, dims, preferred_element_type=F32)


def split(x):
    hi = x.astype(BF)
    return hi, (x - hi.astype(F32)).astype(BF)


def lanes8(x):
    return jnp.concatenate([x] * PER_TILE, axis=1)


def shift(x, amount):
    amount = amount % TILE
    return x if amount == 0 else pltpu.roll(x, amount, 1)


def decays(rate, positions, top=None):
    sub = lax.broadcasted_iota(jnp.int32, (8, TILE), 0).astype(F32)
    blocks = positions // 8
    step = jnp.exp(-8.0 * rate)
    now = jnp.exp(-rate * (sub if top is None else top - (positions - 8) - sub))
    rows = [now]
    for _ in range(blocks - 1):
        now = now * step
        rows.append(now)
    if top is not None:
        rows = rows[::-1]
    return jnp.concatenate(rows, axis=0)


def kernel(
    n_ctx,
    n_z,
    n_tensor,
    n_core,
    n_dp,
    left_hbm,
    right_hbm,
    values_hbm,
    grad_hbm,
    res_hbm,
    rate_hbm,
    vout,
    gout,
    vin,
    par,
    gst,
    tables,
    taps,
    convs,
    msg1,
    recv1,
    msg2,
    recv2,
    grad1,
    gather1,
    grad2,
    gather2,
    in_sem,
    par_sem,
    send_sem,
    recv_sem,
):
    me = lax.axis_index("ctx")
    my_t = lax.axis_index("tensor")
    my_d = lax.axis_index("dp")
    positions = vin.shape[2]
    tiles = vin.shape[1]
    seq = n_ctx * positions
    groups = tiles * PER_TILE
    inv = 1.0 / seq

    for k, ref in enumerate((res_hbm, rate_hbm)):
        pltpu.make_async_copy(ref, gout.at[k], par_sem).start()
    for j in range(tiles):
        for a, ref in enumerate((left_hbm, values_hbm, right_hbm, grad_hbm)):
            pltpu.make_async_copy(
                ref.at[:, pl.ds(j * TILE, TILE)], vin.at[a, j], in_sem
            ).start()

    my_y, my_z = me // n_z, lax.rem(me, n_z)
    my_x, my_c = my_t // n_core, lax.rem(my_t, n_core)
    n_y, n_x = n_ctx // n_z, n_tensor // n_core
    ring = sorted(range(n_y), key=lambda o: -min(o, n_y - o))
    line = [
        (lax.rem(my_y + dy, n_y) * n_z + lax.rem(my_z + dz, n_z))
        for dy in ring
        for dz in reversed(range(n_z))
        if dy or dz
    ]
    first_set = [(peer, {"ctx": peer}) for peer in line]

    def spread(dd, dx, dz):
        d, x, z = lax.rem(my_d + dd, n_dp), lax.rem(my_x + dx, n_x), lax.rem(my_z + dz, n_z)
        where = {"dp": d, "tensor": x * n_core + my_c, "ctx": my_y * n_z + z}
        return (d * n_x + x) * n_z + z, where

    second_set = [
        spread(dd, dx, dz)
        for dd in reversed(range(n_dp))
        for dx in sorted(range(n_x), key=lambda o: -min(o, n_x - o))
        for dz in reversed(range(n_z))
        if dd or dx or dz
    ]
    new_second = [
        where
        for (_, where), (dd, dx) in zip(
            second_set,
            [
                (dd, dx)
                for dd in reversed(range(n_dp))
                for dx in sorted(range(n_x), key=lambda o: -min(o, n_x - o))
                for dz in reversed(range(n_z))
                if dd or dx or dz
            ],
        )
        if dd or dx
    ]

    def across(dy, dc):
        y, c = lax.rem(my_y + dy, n_y), lax.rem(my_c + dc, n_core)
        return c * n_y + y, {"tensor": my_x * n_core + c, "ctx": y * n_z + my_z}

    third_set = [across(dy, dc) for dy in ring for dc in reversed(range(n_core)) if dy or dc]
    new_third = [across(dy, dc)[1] for dy in ring for dc in range(1, n_core)]

    barrier = pltpu.get_barrier_semaphore()
    greeted = [where for _, where in first_set] + new_second + new_third
    for where in greeted:
        pl.semaphore_signal(barrier, inc=1, device_id=where, device_id_type=MESH)

    pltpu.make_async_copy(gout, gout, par_sem).wait()
    for k in range(2):
        par[k] = gout[k].T
    first = pl.multiple_of(my_t * groups, groups)

    lane = lax.broadcasted_iota(jnp.int32, (8, TILE), 1)
    sub = lax.broadcasted_iota(jnp.int32, (8, TILE), 0)
    block = lane // GSIZE
    row_i = lax.broadcasted_iota(jnp.int32, (TILE, TILE), 0)
    col_i = lax.broadcasted_iota(jnp.int32, (TILE, TILE), 1)
    pos_col = row_i.astype(F32)

    slopes = []
    for j in range(tiles):
        pick = pl.ds(pl.multiple_of(first + j * PER_TILE, PER_TILE), PER_TILE)
        rates = jnp.where(block == sub, lanes8(par[1, pick, :]), 0.0)
        resid = jnp.where(block == sub, lanes8(par[0, pick, :]), 0.0)
        rate = jnp.sum(rates, axis=0, keepdims=True) * inv
        ahead = decays(rate, positions, positions)
        ahead1 = decays(shift(rate, 16), positions, positions) * (positions - pos_col)
        after2 = decays(shift(rate, 32), positions) * pos_col
        after = decays(shift(rate, 48), positions)
        q_hi, q_lo = split(ahead)
        p_hi, p_lo = split(after)
        tables[j, 0] = q_hi
        tables[j, 1] = q_lo
        tables[j, 2] = p_hi
        tables[j, 3] = p_lo
        tables[j, 4] = ahead1.astype(BF)
        tables[j, 5] = after2.astype(BF)
        r_hi, r_lo = split(shift(resid, 48))
        taps[j] = dot(r_hi, p_hi, NT) + (dot(r_lo, p_hi, NT) + dot(r_hi, p_lo, NT))

    pltpu.make_async_copy(vin, vin, in_sem).wait()
    mirror = row_i + col_i
    flip = jnp.where(mirror == positions - 1, 1.0, 0.0).astype(BF)
    for j in range(tiles):
        gated = (vin[0, j].astype(F32) * vin[1, j].astype(F32)).astype(BF)
        signal = (vin[2, j].astype(F32) * vin[3, j].astype(F32)).astype(BF)
        gst[0, j] = gated
        gst[1, j] = dot(flip, signal).astype(BF)
        gated_t = gated.T
        signal_t = signal.T
        gst[2, j] = gated_t
        gst[3, j] = signal_t
        kinds = (
            dot(gated_t, tables[j, 0]) + dot(gated_t, tables[j, 1]),
            dot(gated_t, tables[j, 4]),
            dot(signal_t, tables[j, 5]),
            dot(signal_t, tables[j, 2]) + dot(signal_t, tables[j, 3]),
        )
        for g in range(PER_TILE):
            which = (block - g) & 7
            halves = []
            for half in range(2):
                at = g * GSIZE + 8 * half
                part = kinds[3][at : at + 8]
                for k in (2, 1, 0):
                    part = jnp.where(which == k, kinds[k][at : at + 8], part)
                halves.append(part)
            msg1[j * PER_TILE + g, 0:8, :] = jnp.where(
                which < 4, halves[0], shift(halves[1], 64)
            )

    for j in range(tiles):
        gated = gst[0, j]
        flipped = gst[1, j]
        for g in range(PER_TILE):
            only = jnp.where(col_i // GSIZE == g, gated.astype(F32), 0.0).astype(BF)
            pair = jnp.where(mirror < positions, dot(only, flipped, NT), 0.0)
            skew = pltpu.roll(pair, 0, 1, stride=1, stride_axis=0)
            msg1[j * PER_TILE + g, 8:9, :] = jnp.sum(skew, axis=0, keepdims=True)

    def send(src, dst, mine, peers, k):
        for slot, where in peers:
            pltpu.make_async_remote_copy(
                src_ref=src.at[slot] if len(src.shape) == len(dst.shape) else src,
                dst_ref=dst.at[mine],
                send_sem=send_sem.at[k],
                recv_sem=recv_sem.at[k],
                device_id=where,
                device_id_type=MESH,
            ).start()

    def landed(dst, k, peers):
        part = dst.at[pl.ds(0, len(peers))]
        pltpu.make_async_copy(part, part, recv_sem.at[k]).wait()

    def sent(dst, k, peers):
        part = dst.at[pl.ds(0, len(peers))]
        pltpu.make_async_copy(part, part, send_sem.at[k]).wait()

    pl.semaphore_wait(barrier, len(greeted))
    send(msg1, recv1, me, first_set, 0)
    recv1[me] = msg1[me]

    later = col_i >= row_i

    def inside(j, carry):
        rows = taps[j].astype(BF).astype(F32)
        for g in range(PER_TILE):
            wide = jnp.broadcast_to(rows[g : g + 1], (TILE, TILE))
            turned = pltpu.roll(wide, 0, 1, stride=1, stride_axis=0)
            upper = jnp.where(later, turned, 0.0).astype(BF)
            at = g * GSIZE
            convs[0, j, at : at + GSIZE, :] = dot(gst[2, j, at : at + GSIZE, :], upper)
            convs[1, j, at : at + GSIZE, :] = dot(gst[3, j, at : at + GSIZE, :], upper, NT)
        return carry

    lax.fori_loop(0, tiles, inside, 0)

    rate_d = lanes8(par[1, pl.ds(first + me, 1), :]) * inv
    res_d = lanes8(par[0, pl.ds(first + me, 1), :])
    decay_d = decays(rate_d, positions, positions - 1)
    dec = jnp.exp(-rate_d * positions)
    kind = (block - me) & 3
    is0, is1, is2, is3 = [kind == k for k in range(4)]

    landed(recv1, 0, first_set)
    back = jnp.zeros((8, TILE), F32)
    for i in reversed(range(n_ctx)):
        msg2[i] = back
        back = back * dec + recv1[i, 0:8, :]
    front = jnp.zeros((8, TILE), F32)
    sum_r = jnp.zeros((8, TILE), F32)
    sum_s = jnp.zeros((8, TILE), F32)
    sum_m = jnp.zeros((8, TILE), F32)
    for i in range(n_ctx):
        own = recv1[i, 0:8, :]
        behind = msg2[i]
        behind0 = shift(behind, 80)
        own0 = shift(own, 80)
        mixed = shift(jnp.where(is2, own, behind), 96)
        sum_r = sum_r + front * own0
        sum_m = sum_m + front * behind0
        sum_s = sum_s + jnp.where(is0, front, own) * mixed
        msg2[i] = jnp.where(is0, behind0, shift(front, 48)) * res_d
        front = front * dec + own
    send(msg2, recv2, me, first_set, 1)
    recv2[me] = msg2[me]

    def fold(x):
        x = jnp.sum(x, axis=0, keepdims=True)
        return x + shift(x, 64)

    raw_r = fold(sum_r)
    raw_s = fold(jnp.where(is0, sum_s + (positions * dec) * sum_m, 0.0)) + shift(
        fold(jnp.where(is1, sum_s, 0.0)), 112
    )
    lag = jnp.sum(recv1[:, 8:9, :], axis=0)
    weighted = jnp.where(
        sub == 0, lag, jnp.where(sub == 1, lag * (positions - 1 - lane).astype(F32), 0.0)
    )
    shared = lax.dot_general(
        weighted, decay_d, NN, precision=lax.Precision.HIGHEST, preferred_element_type=F32
    )
    raw_r = jnp.where(is0[0:1], raw_r, 0.0)
    raw_s = jnp.where(is0[0:1], raw_s, 0.0)
    raw_r = raw_r + shift(raw_r, 32)
    raw_s = raw_s + shift(raw_s, 32)
    raw_r = raw_r + shift(raw_r, 16) + shared[0:1]
    raw_s = (raw_s + shift(raw_s, 16) + shared[1:2]) * res_d * (-inv)
    grads = jnp.where(block[0:1] % 2 == 0, raw_r, raw_s)
    my_second = (my_d * n_x + my_x) * n_z + my_z
    my_third = my_c * n_y + my_y
    grad1[...] = grads
    send(grad1, gather1, my_second, second_set, 2)
    gather1[my_second] = grads
    landed(gather1, 2, second_set)
    quarter = lax.broadcasted_iota(jnp.int32, (n_z, TILE), 1) // 32
    pack = jnp.zeros((n_z, TILE), F32)
    for x in range(n_x):
        both = gather1[x * n_z : (x + 1) * n_z, 0, :]
        for d in range(1, n_dp):
            at = (d * n_x + x) * n_z
            both = both + gather1[at : at + n_z, 0, :]
        pack = jnp.where(quarter == x, both, pack)
    grad2[...] = pack
    send(grad2, gather2, my_third, third_set, 3)
    gather2[my_third] = pack
    landed(recv2, 1, first_set)

    def finish(j, carry):
        heads = []
        tails = []
        for g in range(PER_TILE):
            m = recv2[j * PER_TILE + g]
            turned = shift(m, 64)
            for part in (m, turned):
                tails.append(jnp.where(block == g, part, 0.0))
                heads.append(jnp.where(block == (g + 3) % 8, part, 0.0))
        h_hi, h_lo = split(jnp.concatenate(heads, axis=0))
        b_hi, b_lo = split(jnp.concatenate(tails, axis=0))
        q_hi, q_lo, p_hi, p_lo = [tables[j, k] for k in range(4)]
        conv = convs[0, j] + (
            dot(h_hi, p_hi, NT) + (dot(h_lo, p_hi, NT) + dot(h_hi, p_lo, NT))
        )
        conv_grad = convs[1, j] + (
            dot(b_hi, q_hi, NT) + (dot(b_lo, q_hi, NT) + dot(b_hi, q_lo, NT))
        )
        conv = conv.astype(BF).T.astype(F32)
        conv_grad = conv_grad.astype(BF).T.astype(F32)
        vout[0, j] = (vin[2, j].astype(F32) * conv).astype(BF)
        vout[1, j] = (conv_grad * vin[1, j].astype(F32)).astype(BF)
        vout[2, j] = (vin[3, j].astype(F32) * conv).astype(BF)
        vout[3, j] = (conv_grad * vin[0, j].astype(F32)).astype(BF)
        return carry

    lax.fori_loop(0, tiles, finish, 0)

    landed(gather2, 3, third_set)
    every = jnp.concatenate([gather2[i] for i in range(n_y * n_core)], axis=0)
    total = jnp.sum(jnp.sum(every * every, axis=0, keepdims=True), axis=1, keepdims=True)
    factor = CLIP / jnp.maximum(jnp.sqrt(total), CLIP)
    turned = (every * factor).T
    span = n_y * n_core * n_z
    for x in range(n_x):
        for k in range(2):
            at = x * 32 + k * ORD
            gout[k, :, x * span : (x + 1) * span] = turned[at : at + ORD]
    sent(recv1, 0, first_set)
    sent(recv2, 1, first_set)
    sent(gather1, 2, second_set)
    sent(gather2, 3, third_set)


def write_out(wide, small, out_conv, out_left, out_right, out_values, out_res, out_rate, sem):
    tiles = wide.shape[1]
    copies = [
        pltpu.make_async_copy(wide.at[a, j], ref.at[:, pl.ds(j * TILE, TILE)], sem)
        for a, ref in enumerate((out_conv, out_left, out_right, out_values))
        for j in range(tiles)
    ] + [pltpu.make_async_copy(small.at[k], ref, sem) for k, ref in enumerate((out_res, out_rate))]
    for copy in copies:
        copy.start()
    pltpu.make_async_copy(wide, wide, sem).wait()
    pltpu.make_async_copy(small, small, sem).wait()


def solution(mesh):
    n_ctx, n_tensor, n_dp = mesh.shape["ctx"], mesh.shape["tensor"], mesh.shape["dp"]

    def on_device(left_gate, right_gate, values, grad_out, residues, decay_rates):
        positions, channels = left_gate.shape[1:]
        tiles = channels // TILE
        groups = channels // GSIZE
        flat = [x.reshape(positions, channels) for x in (left_gate, right_gate, values, grad_out)]
        wide = jax.ShapeDtypeStruct((positions, channels), BF)
        small = jax.ShapeDtypeStruct(residues.shape[::-1], F32)
        in_hbm = pl.BlockSpec(memory_space=pltpu.HBM)
        in_vmem = pl.BlockSpec(memory_space=pltpu.VMEM)
        outs = pl.pallas_call(
            functools.partial(kernel, n_ctx, N_Z, n_tensor, N_CORE, n_dp),
            out_shape=(
                jax.ShapeDtypeStruct((4, tiles, positions, TILE), BF),
                jax.ShapeDtypeStruct((2,) + residues.shape[::-1], F32),
            ),
            in_specs=[in_hbm] * 6,
            out_specs=(in_vmem, in_vmem),
            scratch_shapes=[
                pltpu.VMEM((4, tiles, positions, TILE), BF),
                pltpu.VMEM((2,) + residues.shape, F32),
                pltpu.VMEM((4, tiles, TILE, TILE), BF),
                pltpu.VMEM((tiles, 6, positions, TILE), BF),
                pltpu.VMEM((tiles, PER_TILE, positions), F32),
                pltpu.VMEM((2, tiles, TILE, positions), F32),
                pltpu.VMEM((n_ctx, 9, TILE), F32),
                pltpu.VMEM((n_ctx, 9, TILE), F32),
                pltpu.VMEM((n_ctx, 8, TILE), F32),
                pltpu.VMEM((n_ctx, 8, TILE), F32),
                pltpu.VMEM((1, TILE), F32),
                pltpu.VMEM((n_dp * n_tensor // N_CORE * N_Z, 1, TILE), F32),
                pltpu.VMEM((N_Z, TILE), F32),
                pltpu.VMEM((n_ctx // N_Z * N_CORE, N_Z, TILE), F32),
                pltpu.SemaphoreType.DMA,
                pltpu.SemaphoreType.DMA,
                pltpu.SemaphoreType.DMA((4,)),
                pltpu.SemaphoreType.DMA((4,)),
            ],
            compiler_params=pltpu.CompilerParams(
                collective_id=0, has_side_effects=True, vmem_limit_bytes=16 * 1024 * 1024
            ),
        )(*[pltpu.with_memory_space_constraint(x, pltpu.HBM) for x in (*flat, residues.T, decay_rates.T)])
        outs = pl.pallas_call(
            write_out,
            out_shape=(wide, wide, wide, wide, small, small),
            in_specs=[pl.BlockSpec(memory_space=pl.ANY)] * 2,
            out_specs=(in_hbm,) * 6,
            scratch_shapes=[pltpu.SemaphoreType.DMA],
            compiler_params=pltpu.CompilerParams(vmem_limit_bytes=1024 * 1024),
        )(*outs)
        full = [x.reshape(1, positions, channels) for x in outs[:4]]
        return (*full, outs[4].T, outs[5].T)

    wide = P("dp", "ctx", "tensor")
    return jax.shard_map(
        on_device,
        mesh=mesh,
        in_specs=(wide, wide, wide, wide, P(), P()),
        out_specs=(wide, wide, wide, wide, P(), P()),
        check_vma=False,
    )
```

```python
import functools

import jax
import jax.numpy as jnp
from jax import lax
from jax.experimental import pallas as pl
from jax.experimental.pallas import tpu as pltpu
from jax.sharding import PartitionSpec as P

MESH = pl.DeviceIdType.MESH
BF = jnp.bfloat16
F32 = jnp.float32
GSIZE = 16
ORD = 16
TILE = 128
PER_TILE = TILE // GSIZE
CLIP = 32.0
N_Z = 4
N_CORE = 2
NT = (((1,), (1,)), ((), ()))
NN = (((1,), (0,)), ((), ()))


def dot(a, b, dims=NN):
    return lax.dot_general(a, b, dims, preferred_element_type=F32)


def split(x):
    hi = x.astype(BF)
    return hi, (x - hi.astype(F32)).astype(BF)


def lanes8(x):
    return jnp.concatenate([x] * PER_TILE, axis=1)


def shift(x, amount):
    amount = amount % TILE
    return x if amount == 0 else pltpu.roll(x, amount, 1)


def decays(rate, positions, top=None):
    sub = lax.broadcasted_iota(jnp.int32, (8, TILE), 0).astype(F32)
    blocks = positions // 8
    step = jnp.exp(-8.0 * rate)
    now = jnp.exp(-rate * (sub if top is None else top - (positions - 8) - sub))
    rows = [now]
    for _ in range(blocks - 1):
        now = now * step
        rows.append(now)
    if top is not None:
        rows = rows[::-1]
    return jnp.concatenate(rows, axis=0)


def kernel(
    n_ctx,
    n_z,
    n_tensor,
    n_core,
    n_dp,
    left_hbm,
    right_hbm,
    values_hbm,
    grad_hbm,
    res_hbm,
    rate_hbm,
    vout,
    gout,
    vin,
    par,
    gst,
    tables,
    taps,
    convs,
    msg1,
    recv1,
    hold,
    msg2,
    recv2,
    grad1,
    gather1,
    grad2,
    gather2,
    in_sem,
    par_sem,
    send_sem,
    recv_sem,
):
    me = lax.axis_index("ctx")
    my_t = lax.axis_index("tensor")
    my_d = lax.axis_index("dp")
    positions = vin.shape[1]
    tiles = vin.shape[2] // TILE
    seq = n_ctx * positions
    groups = tiles * PER_TILE
    inv = 1.0 / seq

    my_y, my_z = me // n_z, lax.rem(me, n_z)
    my_x, my_c = my_t // n_core, lax.rem(my_t, n_core)
    n_y, n_x = n_ctx // n_z, n_tensor // n_core
    ring = sorted(range(n_y), key=lambda o: -min(o, n_y - o))
    line = [
        (lax.rem(my_y + dy, n_y) * n_z + lax.rem(my_z + dz, n_z))
        for dy in ring
        for dz in reversed(range(n_z))
        if dy or dz
    ]
    mids = tuple(range(1, n_z - 1))
    n_mid = len(mids)
    own = (my_z >= mids[0]) & (my_z <= mids[-1])
    held = groups // (n_y * n_mid)
    my_owner = my_y * n_mid + my_z - mids[0]

    def owner(dy, m):
        y = lax.rem(my_y + dy, n_y)
        return y * n_mid + m - mids[0], y * n_z + m

    owners = [owner(dy, m) for dy in ring if dy for m in mids]
    near = [owner(0, m) for m in mids]

    def spread(dd, dx, z):
        d, x = lax.rem(my_d + dd, n_dp), lax.rem(my_x + dx, n_x)
        return {"dp": d, "tensor": x * n_core + my_c, "ctx": my_y * n_z + z}

    turns = [
        (dd, dx)
        for dd in reversed(range(n_dp))
        for dx in sorted(range(n_x), key=lambda o: -min(o, n_x - o))
    ]
    second_set = [
        spread(dd, dx, lax.rem(my_z + dz, n_z))
        for dd, dx in turns
        for dz in reversed(range(n_z))
        if dd or dx or dz
    ]

    def across(dy, dc):
        y, c = lax.rem(my_y + dy, n_y), lax.rem(my_c + dc, n_core)
        return c * n_y + y, {"tensor": my_x * n_core + c, "ctx": y * n_z + my_z}

    third_set = [across(dy, dc)[1] for dy in ring for dc in reversed(range(n_core)) if dy or dc]

    barrier = pltpu.get_barrier_semaphore()

    def greet(where):
        pl.semaphore_signal(barrier, inc=1, device_id=where, device_id_type=MESH)

    ends = (0, n_z - 1)

    @pl.when(own)
    def _():
        for dy in ring:
            for z in ends:
                greet({"ctx": lax.rem(my_y + dy, n_y) * n_z + z})
        for dd, dx in turns:
            if dd or dx:
                for z in ends:
                    greet(spread(dd, dx, z))
        greet({"ctx": my_y * n_z + mids[0] + mids[-1] - my_z})

    for _, peer in owners:
        greet({"ctx": peer})
    for dd, dx in turns:
        if dd or dx:
            for z in mids:
                greet(spread(dd, dx, z))
    for dy in ring:
        for dc in range(1, n_core):
            greet(across(dy, dc)[1])

    @pl.when(jnp.logical_not(own))
    def _():
        for dy in ring:
            if dy:
                greet(across(dy, 0)[1])
        for _, peer in near:
            greet({"ctx": peer})

    n_side = n_dp * n_x
    met_own = n_ctx - 1 + (n_side - 1) * n_z + n_y * (n_core - 1)
    met_end = n_y * n_mid + (n_side - 1) * n_mid + n_y * n_core - 1
    met = jnp.where(own, met_own, met_end)

    for k, ref in enumerate((res_hbm, rate_hbm)):
        pltpu.make_async_copy(ref, gout.at[k], par_sem).start()
    for a, ref in enumerate((left_hbm, values_hbm, right_hbm, grad_hbm)):
        pltpu.make_async_copy(ref, vin.at[a], in_sem).start()
    pltpu.make_async_copy(gout, gout, par_sem).wait()
    for k in range(2):
        par[k] = gout[k].T
    first = pl.multiple_of(my_t * groups, groups)

    lane = lax.broadcasted_iota(jnp.int32, (8, TILE), 1)
    sub = lax.broadcasted_iota(jnp.int32, (8, TILE), 0)
    block = lane // GSIZE
    row_i = lax.broadcasted_iota(jnp.int32, (TILE, TILE), 0)
    col_i = lax.broadcasted_iota(jnp.int32, (TILE, TILE), 1)
    pos_col = row_i.astype(F32)

    slopes = []
    for j in range(tiles):
        pick = pl.ds(pl.multiple_of(first + j * PER_TILE, PER_TILE), PER_TILE)
        rates = jnp.where(block == sub, lanes8(par[1, pick, :]), 0.0)
        resid = jnp.where(block == sub, lanes8(par[0, pick, :]), 0.0)
        rate = jnp.sum(rates, axis=0, keepdims=True) * inv
        ahead = decays(rate, positions, positions)
        ahead1 = decays(shift(rate, 16), positions, positions) * (positions - pos_col)
        after2 = decays(shift(rate, 32), positions) * pos_col
        after = decays(shift(rate, 48), positions)
        q_hi, q_lo = split(ahead)
        p_hi, p_lo = split(after)
        tables[j, 0] = q_hi
        tables[j, 1] = q_lo
        tables[j, 2] = p_hi
        tables[j, 3] = p_lo
        tables[j, 4] = ahead1.astype(BF)
        tables[j, 5] = after2.astype(BF)
        r_hi, r_lo = split(shift(resid, 48))
        taps[j] = dot(r_hi, p_hi, NT) + (dot(r_lo, p_hi, NT) + dot(r_hi, p_lo, NT))

    pltpu.make_async_copy(vin, vin, in_sem).wait()
    mirror = row_i + col_i
    flip = jnp.where(mirror == positions - 1, 1.0, 0.0).astype(BF)
    for j in range(tiles):
        gated = (vin[0, :, j * TILE : (j + 1) * TILE].astype(F32) * vin[1, :, j * TILE : (j + 1) * TILE].astype(F32)).astype(BF)
        signal = (vin[2, :, j * TILE : (j + 1) * TILE].astype(F32) * vin[3, :, j * TILE : (j + 1) * TILE].astype(F32)).astype(BF)
        gst[0, j] = gated
        gst[1, j] = dot(flip, signal).astype(BF)
        gated_t = gated.T
        signal_t = signal.T
        gst[2, j] = gated_t
        gst[3, j] = signal_t
        kinds = (
            dot(gated_t, tables[j, 0]) + dot(gated_t, tables[j, 1]),
            dot(gated_t, tables[j, 4]),
            dot(signal_t, tables[j, 5]),
            dot(signal_t, tables[j, 2]) + dot(signal_t, tables[j, 3]),
        )
        for g in range(PER_TILE):
            which = (block - g) & 7
            halves = []
            for half in range(2):
                at = g * GSIZE + 8 * half
                part = kinds[3][at : at + 8]
                for k in (2, 1, 0):
                    part = jnp.where(which == k, kinds[k][at : at + 8], part)
                halves.append(part)
            msg1[j * PER_TILE + g, 0:8, :] = jnp.where(
                which < 4, halves[0], shift(halves[1], 64)
            )

    for j in range(tiles):
        gated = gst[0, j]
        flipped = gst[1, j]
        for g in range(PER_TILE):
            only = jnp.where(col_i // GSIZE == g, gated.astype(F32), 0.0).astype(BF)
            pair = jnp.where(mirror < positions, dot(only, flipped, NT), 0.0)
            skew = pltpu.roll(pair, 0, 1, stride=1, stride_axis=0)
            msg1[j * PER_TILE + g, 8:9, :] = jnp.sum(skew, axis=0, keepdims=True)

    def send(src, dst, where, k):
        pltpu.make_async_remote_copy(
            src_ref=src,
            dst_ref=dst,
            send_sem=send_sem.at[k],
            recv_sem=recv_sem.at[k],
            device_id=where,
            device_id_type=MESH,
        ).start()

    def settle(sem, dst, count):
        part = dst.at[pl.ds(0, count)]
        pltpu.make_async_copy(part, part, sem).wait()

    def by_role(sem, dst, count_own, count_end):
        @pl.when(own)
        def _():
            settle(sem, dst, count_own)

        @pl.when(jnp.logical_not(own))
        def _():
            settle(sem, dst, count_end)

    n_owner = n_y * n_mid

    pl.semaphore_wait(barrier, met)
    for o, peer in owners:
        send(msg1.at[pl.ds(held * o, held)], recv1.at[me], {"ctx": peer}, 0)
    for o, peer in near:

        @pl.when(peer != me)
        def _():
            send(msg1.at[pl.ds(held * o, held)], recv1.at[me], {"ctx": peer}, 0)

    later = col_i >= row_i

    def inside(j, carry):
        rows = taps[j].astype(BF).astype(F32)
        for g in range(PER_TILE):
            wide = jnp.broadcast_to(rows[g : g + 1], (TILE, TILE))
            turned = pltpu.roll(wide, 0, 1, stride=1, stride_axis=0)
            upper = jnp.where(later, turned, 0.0).astype(BF)
            at = g * GSIZE
            convs[0, j, at : at + GSIZE, :] = dot(gst[2, j, at : at + GSIZE, :], upper)
            convs[1, j, at : at + GSIZE, :] = dot(gst[3, j, at : at + GSIZE, :], upper, NT)
        return carry

    lax.fori_loop(0, tiles, inside, 0)

    @pl.when(own)
    def _():
        recv1[me] = msg1[pl.ds(held * my_owner, held)]
        local = []
        for k in range(held):
            at = held * my_owner + k
            rate_d = lanes8(par[1, pl.ds(first + at, 1), :]) * inv
            res_d = lanes8(par[0, pl.ds(first + at, 1), :])
            decay_d = decays(rate_d, positions, positions - 1)
            local.append((rate_d, res_d, decay_d, (block - at) & 3))
        settle(recv_sem.at[0], recv1, n_ctx - 1)
        for k in range(held):
            rate_d, res_d, decay_d, kind = local[k]
            dec = jnp.exp(-rate_d * positions)
            is0, is1, is2, is3 = [kind == v for v in range(4)]
            outer = is0 | is3
            back = jnp.zeros((8, TILE), F32)
            for i in reversed(range(n_ctx)):
                hold[k, i] = back
                back = back * dec + recv1[i, k, 0:8, :]
            front = jnp.zeros((8, TILE), F32)
            sum_r = jnp.zeros((8, TILE), F32)
            sum_s = jnp.zeros((8, TILE), F32)
            sum_m = jnp.zeros((8, TILE), F32)
            for i in range(n_ctx):
                mine = recv1[i, k, 0:8, :]
                behind = hold[k, i]
                behind0 = shift(behind, 80)
                mixed = shift(jnp.where(is2, mine, behind), 96)
                sum_r = sum_r + front * shift(mine, 80)
                sum_m = sum_m + front * behind0
                sum_s = sum_s + jnp.where(is0, front, mine) * mixed
                both = jnp.where(is0, behind0, shift(front, 48)) * res_d
                low = shift(pltpu.roll(both, 4, 0), 32)
                msg2[i, k] = jnp.where(outer, both, low)[0:4]
                front = front * dec + mine

            def fold(x):
                x = jnp.sum(x, axis=0, keepdims=True)
                return x + shift(x, 64)

            raw_r = fold(sum_r)
            raw_s = fold(jnp.where(is0, sum_s + (positions * dec) * sum_m, 0.0)) + shift(
                fold(jnp.where(is1, sum_s, 0.0)), 112
            )
            lag = jnp.sum(recv1[:, k, 8:9, :], axis=0)
            weighted = jnp.where(
                sub == 0, lag, jnp.where(sub == 1, lag * (positions - 1 - lane).astype(F32), 0.0)
            )
            shared = lax.dot_general(
                weighted, decay_d, NN, precision=lax.Precision.HIGHEST, preferred_element_type=F32
            )
            raw_r = jnp.where(is0[0:1], raw_r, 0.0)
            raw_s = jnp.where(is0[0:1], raw_s, 0.0)
            raw_r = raw_r + shift(raw_r, 32)
            raw_s = raw_s + shift(raw_s, 32)
            raw_r = raw_r + shift(raw_r, 16) + shared[0:1]
            raw_s = (raw_s + shift(raw_s, 16) + shared[1:2]) * res_d * (-inv)
            grad1[k] = jnp.where(block[0:1] % 2 == 0, raw_r, raw_s)
        slot = ((my_d * n_x + my_x) * n_mid + my_z - mids[0]) * held
        for where in second_set:
            send(grad1, gather1.at[pl.ds(slot, held)], where, 2)
        gather1[pl.ds(slot, held)] = grad1[...]
        for peer in line:
            send(msg2.at[peer], recv2.at[my_owner], {"ctx": peer}, 1)
        recv2[my_owner] = msg2[me]

    n_second = n_side * n_mid

    @pl.when(own)
    def _():
        settle(recv_sem.at[2], gather1, (n_second - 1) * held)

    @pl.when(jnp.logical_not(own))
    def _():
        settle(recv_sem.at[2], gather1, n_second * held)

    quarter = lax.broadcasted_iota(jnp.int32, (n_z, TILE), 1) // 32
    pack = jnp.zeros((n_z, TILE), F32)
    for x in range(n_x):
        both = gather1[x * n_z : (x + 1) * n_z, 0, :]
        for d in range(1, n_dp):
            at = (d * n_x + x) * n_z
            both = both + gather1[at : at + n_z, 0, :]
        pack = jnp.where(quarter == x, both, pack)
    grad2[...] = pack
    my_third = my_c * n_y + my_y
    for where in third_set:
        send(grad2, gather2.at[my_third], where, 3)
    gather2[my_third] = pack
    by_role(recv_sem.at[1], recv2, n_owner - 1, n_owner)

    def finish(j, carry):
        heads = []
        tails = []
        for g in range(PER_TILE):
            at = j * PER_TILE + g
            top = recv2[at // held, at % held]
            m = jnp.concatenate([top, shift(top, 96)], axis=0)
            turned = shift(m, 64)
            for part in (m, turned):
                tails.append(jnp.where(block == g, part, 0.0))
                heads.append(jnp.where(block == (g + 3) % 8, part, 0.0))
        h_hi, h_lo = split(jnp.concatenate(heads, axis=0))
        b_hi, b_lo = split(jnp.concatenate(tails, axis=0))
        q_hi, q_lo, p_hi, p_lo = [tables[j, k] for k in range(4)]
        conv = convs[0, j] + (
            dot(h_hi, p_hi, NT) + (dot(h_lo, p_hi, NT) + dot(h_hi, p_lo, NT))
        )
        conv_grad = convs[1, j] + (
            dot(b_hi, q_hi, NT) + (dot(b_lo, q_hi, NT) + dot(b_hi, q_lo, NT))
        )
        conv = conv.astype(BF).T.astype(F32)
        conv_grad = conv_grad.astype(BF).T.astype(F32)
        vout[0, :, j * TILE : (j + 1) * TILE] = (vin[2, :, j * TILE : (j + 1) * TILE].astype(F32) * conv).astype(BF)
        vout[1, :, j * TILE : (j + 1) * TILE] = (conv_grad * vin[1, :, j * TILE : (j + 1) * TILE].astype(F32)).astype(BF)
        vout[2, :, j * TILE : (j + 1) * TILE] = (vin[3, :, j * TILE : (j + 1) * TILE].astype(F32) * conv).astype(BF)
        vout[3, :, j * TILE : (j + 1) * TILE] = (conv_grad * vin[0, :, j * TILE : (j + 1) * TILE].astype(F32)).astype(BF)
        return carry

    for j in range(tiles):
        finish(j, 0)

    settle(recv_sem.at[3], gather2, len(third_set))
    every = jnp.concatenate([gather2[i] for i in range(n_y * n_core)], axis=0)
    total = jnp.sum(jnp.sum(every * every, axis=0, keepdims=True), axis=1, keepdims=True)
    factor = CLIP / jnp.maximum(jnp.sqrt(total), CLIP)
    turned = (every * factor).T
    span = n_y * n_core * n_z
    for x in range(n_x):
        for k in range(2):
            at = x * 32 + k * ORD
            gout[k, :, x * span : (x + 1) * span] = turned[at : at + ORD]
    by_role(send_sem.at[0], recv1, n_owner - 1, n_owner)

    @pl.when(own)
    def _():
        settle(send_sem.at[1], msg2, n_ctx - 1)
        settle(send_sem.at[2], gather1, len(second_set) * held)

    settle(send_sem.at[3], gather2, len(third_set))


def write_out(wide, small, out_conv, out_left, out_right, out_values, out_res, out_rate, sem):
    copies = [
        pltpu.make_async_copy(src, ref, sem)
        for src, ref in (
            (small.at[0], out_res),
            (small.at[1], out_rate),
            (wide.at[0], out_conv),
            (wide.at[1], out_left),
            (wide.at[2], out_right),
            (wide.at[3], out_values),
        )
    ]
    for copy in copies:
        copy.start()
    pltpu.make_async_copy(wide, wide, sem).wait()
    pltpu.make_async_copy(small, small, sem).wait()


def solution(mesh):
    n_ctx, n_tensor, n_dp = mesh.shape["ctx"], mesh.shape["tensor"], mesh.shape["dp"]

    def on_device(left_gate, right_gate, values, grad_out, residues, decay_rates):
        positions, channels = left_gate.shape[1:]
        tiles = channels // TILE
        groups = channels // GSIZE
        held = groups // (n_ctx // N_Z * (N_Z - 2))
        flat = [x.reshape(positions, channels) for x in (left_gate, right_gate, values, grad_out)]
        wide = jax.ShapeDtypeStruct((positions, channels), BF)
        small = jax.ShapeDtypeStruct(residues.shape[::-1], F32)
        in_hbm = pl.BlockSpec(memory_space=pltpu.HBM)
        in_vmem = pl.BlockSpec(memory_space=pltpu.VMEM)
        outs = pl.pallas_call(
            functools.partial(kernel, n_ctx, N_Z, n_tensor, N_CORE, n_dp),
            out_shape=(
                jax.ShapeDtypeStruct((4, positions, channels), BF),
                jax.ShapeDtypeStruct((2,) + residues.shape[::-1], F32),
            ),
            in_specs=[in_hbm] * 6,
            out_specs=(in_vmem, in_vmem),
            scratch_shapes=[
                pltpu.VMEM((4, positions, channels), BF),
                pltpu.VMEM((2,) + residues.shape, F32),
                pltpu.VMEM((4, tiles, TILE, TILE), BF),
                pltpu.VMEM((tiles, 6, positions, TILE), BF),
                pltpu.VMEM((tiles, PER_TILE, positions), F32),
                pltpu.VMEM((2, tiles, TILE, positions), F32),
                pltpu.VMEM((groups, 9, TILE), F32),
                pltpu.VMEM((n_ctx, held, 9, TILE), F32),
                pltpu.VMEM((held, n_ctx, 8, TILE), F32),
                pltpu.VMEM((n_ctx, held, 4, TILE), F32),
                pltpu.VMEM((groups // held, held, 4, TILE), F32),
                pltpu.VMEM((held, 1, TILE), F32),
                pltpu.VMEM((n_dp * n_tensor // N_CORE * N_Z * held, 1, TILE), F32),
                pltpu.VMEM((N_Z, TILE), F32),
                pltpu.VMEM((n_ctx // N_Z * N_CORE, N_Z, TILE), F32),
                pltpu.SemaphoreType.DMA,
                pltpu.SemaphoreType.DMA,
                pltpu.SemaphoreType.DMA((4,)),
                pltpu.SemaphoreType.DMA((4,)),
            ],
            compiler_params=pltpu.CompilerParams(
                collective_id=0, has_side_effects=True, vmem_limit_bytes=16 * 1024 * 1024
            ),
        )(*[pltpu.with_memory_space_constraint(x, pltpu.HBM) for x in (*flat, residues.T, decay_rates.T)])
        outs = pl.pallas_call(
            write_out,
            out_shape=(wide, wide, wide, wide, small, small),
            in_specs=[pl.BlockSpec(memory_space=pl.ANY)] * 2,
            out_specs=(in_hbm,) * 6,
            scratch_shapes=[pltpu.SemaphoreType.DMA],
            compiler_params=pltpu.CompilerParams(vmem_limit_bytes=1024 * 1024),
        )(*outs)
        full = [x.reshape(1, positions, channels) for x in outs[:4]]
        return (*full, outs[4].T, outs[5].T)

    wide = P("dp", "ctx", "tensor")
    return jax.shard_map(
        on_device,
        mesh=mesh,
        in_specs=(wide, wide, wide, wide, P(), P()),
        out_specs=(wide, wide, wide, wide, P(), P()),
        check_vma=False,
    )
```

```python
import functools

import jax
import jax.numpy as jnp
from jax import lax
from jax.experimental import pallas as pl
from jax.experimental.pallas import tpu as pltpu
from jax.sharding import PartitionSpec as P

MESH = pl.DeviceIdType.MESH
BF = jnp.bfloat16
F32 = jnp.float32
GSIZE = 16
ORD = 16
TILE = 128
PER_TILE = TILE // GSIZE
CLIP = 32.0
N_Z = 4
N_CORE = 2
NT = (((1,), (1,)), ((), ()))
NN = (((1,), (0,)), ((), ()))


def dot(a, b, dims=NN):
    return lax.dot_general(a, b, dims, preferred_element_type=F32)


def split(x):
    hi = x.astype(BF)
    return hi, (x - hi.astype(F32)).astype(BF)


def lanes8(x):
    return jnp.concatenate([x] * PER_TILE, axis=1)


def shift(x, amount):
    amount = amount % TILE
    return x if amount == 0 else pltpu.roll(x, amount, 1)


def decays(rate, positions, top=None):
    sub = lax.broadcasted_iota(jnp.int32, (8, TILE), 0).astype(F32)
    blocks = positions // 8
    step = jnp.exp(-8.0 * rate)
    now = jnp.exp(-rate * (sub if top is None else top - (positions - 8) - sub))
    rows = [now]
    for _ in range(blocks - 1):
        now = now * step
        rows.append(now)
    if top is not None:
        rows = rows[::-1]
    return jnp.concatenate(rows, axis=0)


def kernel(
    n_ctx,
    n_z,
    n_tensor,
    n_core,
    n_dp,
    left_hbm,
    right_hbm,
    values_hbm,
    grad_hbm,
    res_hbm,
    rate_hbm,
    vout,
    gout,
    vin,
    par,
    gst,
    tables,
    taps,
    convs,
    msg1,
    recv1,
    hold,
    fronts,
    msg2,
    recv2,
    grad1,
    gather1,
    grad2,
    gather2,
    in_sem,
    par_sem,
    send_sem,
    recv_sem,
):
    me = lax.axis_index("ctx")
    my_t = lax.axis_index("tensor")
    my_d = lax.axis_index("dp")
    positions = vin.shape[1]
    tiles = vin.shape[2] // TILE
    seq = n_ctx * positions
    groups = tiles * PER_TILE
    inv = 1.0 / seq

    my_y, my_z = me // n_z, lax.rem(me, n_z)
    my_x, my_c = my_t // n_core, lax.rem(my_t, n_core)
    n_y, n_x = n_ctx // n_z, n_tensor // n_core
    ring = sorted(range(n_y), key=lambda o: -min(o, n_y - o))
    line = [
        (lax.rem(my_y + dy, n_y) * n_z + lax.rem(my_z + dz, n_z))
        for dy in ring
        for dz in reversed(range(n_z))
        if dy or dz
    ]
    mids = tuple(range(1, n_z - 1))
    n_mid = len(mids)
    own = (my_z >= mids[0]) & (my_z <= mids[-1])
    held = groups // (n_y * n_mid)
    my_owner = my_y * n_mid + my_z - mids[0]

    def owner(dy, m):
        y = lax.rem(my_y + dy, n_y)
        return y * n_mid + m - mids[0], y * n_z + m

    owners = [owner(dy, m) for dy in ring if dy for m in mids]
    near = [owner(0, m) for m in mids]

    def spread(dd, dx, z):
        d, x = lax.rem(my_d + dd, n_dp), lax.rem(my_x + dx, n_x)
        return {"dp": d, "tensor": x * n_core + my_c, "ctx": my_y * n_z + z}

    turns = [
        (dd, dx)
        for dd in reversed(range(n_dp))
        for dx in sorted(range(n_x), key=lambda o: -min(o, n_x - o))
    ]
    second_set = [
        spread(dd, dx, lax.rem(my_z + dz, n_z))
        for dd, dx in turns
        for dz in reversed(range(n_z))
        if dd or dx or dz
    ]

    def across(dy, dc):
        y, c = lax.rem(my_y + dy, n_y), lax.rem(my_c + dc, n_core)
        return c * n_y + y, {"tensor": my_x * n_core + c, "ctx": y * n_z + my_z}

    third_set = [across(dy, dc)[1] for dy in ring for dc in reversed(range(n_core)) if dy or dc]

    barrier = pltpu.get_barrier_semaphore()

    def greet(where):
        pl.semaphore_signal(barrier, inc=1, device_id=where, device_id_type=MESH)

    ends = (0, n_z - 1)

    @pl.when(own)
    def _():
        for dy in ring:
            for z in ends:
                greet({"ctx": lax.rem(my_y + dy, n_y) * n_z + z})
        for dd, dx in turns:
            if dd or dx:
                for z in ends:
                    greet(spread(dd, dx, z))
        greet({"ctx": my_y * n_z + mids[0] + mids[-1] - my_z})

    for _, peer in owners:
        greet({"ctx": peer})
    for dd, dx in turns:
        if dd or dx:
            for z in mids:
                greet(spread(dd, dx, z))
    for dy in ring:
        for dc in range(1, n_core):
            greet(across(dy, dc)[1])

    @pl.when(jnp.logical_not(own))
    def _():
        for dy in ring:
            if dy:
                greet(across(dy, 0)[1])
        for _, peer in near:
            greet({"ctx": peer})

    n_side = n_dp * n_x
    met_own = n_ctx - 1 + (n_side - 1) * n_z + n_y * (n_core - 1)
    met_end = n_y * n_mid + (n_side - 1) * n_mid + n_y * n_core - 1
    met = jnp.where(own, met_own, met_end)

    for k, ref in enumerate((res_hbm, rate_hbm)):
        pltpu.make_async_copy(ref, gout.at[k], par_sem).start()
    for a, ref in enumerate((left_hbm, values_hbm, right_hbm, grad_hbm)):
        pltpu.make_async_copy(ref, vin.at[a], in_sem).start()
    pltpu.make_async_copy(gout, gout, par_sem).wait()
    for k in range(2):
        par[k] = gout[k].T
    first = pl.multiple_of(my_t * groups, groups)

    lane = lax.broadcasted_iota(jnp.int32, (8, TILE), 1)
    sub = lax.broadcasted_iota(jnp.int32, (8, TILE), 0)
    block = lane // GSIZE
    row_i = lax.broadcasted_iota(jnp.int32, (TILE, TILE), 0)
    col_i = lax.broadcasted_iota(jnp.int32, (TILE, TILE), 1)
    pos_col = row_i.astype(F32)

    slopes = []
    for j in range(tiles):
        pick = pl.ds(pl.multiple_of(first + j * PER_TILE, PER_TILE), PER_TILE)
        rates = jnp.where(block == sub, lanes8(par[1, pick, :]), 0.0)
        resid = jnp.where(block == sub, lanes8(par[0, pick, :]), 0.0)
        rate = jnp.sum(rates, axis=0, keepdims=True) * inv
        ahead = decays(rate, positions, positions)
        ahead1 = decays(shift(rate, 16), positions, positions) * (positions - pos_col)
        after2 = decays(shift(rate, 32), positions) * pos_col
        after = decays(shift(rate, 48), positions)
        q_hi, q_lo = split(ahead)
        p_hi, p_lo = split(after)
        tables[j, 0] = q_hi
        tables[j, 1] = q_lo
        tables[j, 2] = p_hi
        tables[j, 3] = p_lo
        tables[j, 4] = ahead1.astype(BF)
        tables[j, 5] = after2.astype(BF)
        r_hi, r_lo = split(shift(resid, 48))
        taps[j] = dot(r_hi, p_hi, NT) + (dot(r_lo, p_hi, NT) + dot(r_hi, p_lo, NT))

    pltpu.make_async_copy(vin, vin, in_sem).wait()
    mirror = row_i + col_i
    flip = jnp.where(mirror == positions - 1, 1.0, 0.0).astype(BF)
    for j in range(tiles):
        gated = (vin[0, :, j * TILE : (j + 1) * TILE].astype(F32) * vin[1, :, j * TILE : (j + 1) * TILE].astype(F32)).astype(BF)
        signal = (vin[2, :, j * TILE : (j + 1) * TILE].astype(F32) * vin[3, :, j * TILE : (j + 1) * TILE].astype(F32)).astype(BF)
        gst[0, j] = gated
        gst[1, j] = dot(flip, signal).astype(BF)
        gated_t = gated.T
        signal_t = signal.T
        gst[2, j] = gated_t
        gst[3, j] = signal_t
        kinds = (
            dot(gated_t, tables[j, 0]) + dot(gated_t, tables[j, 1]),
            dot(gated_t, tables[j, 4]),
            dot(signal_t, tables[j, 5]),
            dot(signal_t, tables[j, 2]) + dot(signal_t, tables[j, 3]),
        )
        for g in range(PER_TILE):
            which = (block - g) & 7
            halves = []
            for half in range(2):
                at = g * GSIZE + 8 * half
                part = kinds[3][at : at + 8]
                for k in (2, 1, 0):
                    part = jnp.where(which == k, kinds[k][at : at + 8], part)
                halves.append(part)
            msg1[j * PER_TILE + g, 0:8, :] = jnp.where(
                which < 4, halves[0], shift(halves[1], 64)
            )

    for j in range(tiles):
        gated = gst[0, j]
        flipped = gst[1, j]
        for g in range(PER_TILE):
            only = jnp.where(col_i // GSIZE == g, gated.astype(F32), 0.0).astype(BF)
            pair = jnp.where(mirror < positions, dot(only, flipped, NT), 0.0)
            skew = pltpu.roll(pair, 0, 1, stride=1, stride_axis=0)
            msg1[j * PER_TILE + g, 8:9, :] = jnp.sum(skew, axis=0, keepdims=True)

    def send(src, dst, where, k):
        pltpu.make_async_remote_copy(
            src_ref=src,
            dst_ref=dst,
            send_sem=send_sem.at[k],
            recv_sem=recv_sem.at[k],
            device_id=where,
            device_id_type=MESH,
        ).start()

    def settle(sem, dst, count):
        part = dst.at[pl.ds(0, count)]
        pltpu.make_async_copy(part, part, sem).wait()

    def by_role(sem, dst, count_own, count_end):
        @pl.when(own)
        def _():
            settle(sem, dst, count_own)

        @pl.when(jnp.logical_not(own))
        def _():
            settle(sem, dst, count_end)

    n_owner = n_y * n_mid

    pl.semaphore_wait(barrier, met)
    for o, peer in owners:
        send(msg1.at[pl.ds(held * o, held)], recv1.at[me], {"ctx": peer}, 0)
    for o, peer in near:

        @pl.when(peer != me)
        def _():
            send(msg1.at[pl.ds(held * o, held)], recv1.at[me], {"ctx": peer}, 0)

    later = col_i >= row_i

    def inside(j, carry):
        rows = taps[j].astype(BF).astype(F32)
        for g in range(PER_TILE):
            wide = jnp.broadcast_to(rows[g : g + 1], (TILE, TILE))
            turned = pltpu.roll(wide, 0, 1, stride=1, stride_axis=0)
            upper = jnp.where(later, turned, 0.0).astype(BF)
            at = g * GSIZE
            convs[0, j, at : at + GSIZE, :] = dot(gst[2, j, at : at + GSIZE, :], upper)
            convs[1, j, at : at + GSIZE, :] = dot(gst[3, j, at : at + GSIZE, :], upper, NT)
        return carry

    lax.fori_loop(0, tiles, inside, 0)

    @pl.when(own)
    def _():
        recv1[me] = msg1[pl.ds(held * my_owner, held)]
        local = []
        for k in range(held):
            at = held * my_owner + k
            rate_d = lanes8(par[1, pl.ds(first + at, 1), :]) * inv
            res_d = lanes8(par[0, pl.ds(first + at, 1), :])
            decay_d = decays(rate_d, positions, positions - 1)
            local.append((rate_d, res_d, decay_d, (block - at) & 3))
        settle(recv_sem.at[0], recv1, n_ctx - 1)
        zero = jnp.zeros((8, TILE), F32)
        decs = [jnp.exp(-local[k][0] * positions) for k in range(held)]
        back = [zero] * held
        for i in reversed(range(n_ctx)):
            for k in range(held):
                hold[k, i] = back[k]
                back[k] = back[k] * decs[k] + recv1[i, k, 0:8, :]
        front, sums_r, sums_s, sums_m = [zero] * held, [zero] * held, [zero] * held, [zero] * held
        for i in range(n_ctx):
            for k in range(held):
                kind = local[k][3]
                mine = recv1[i, k, 0:8, :]
                behind = hold[k, i]
                mixed = shift(jnp.where(kind == 2, mine, behind), 96)
                sums_r[k] = sums_r[k] + front[k] * shift(mine, 80)
                sums_m[k] = sums_m[k] + front[k] * shift(behind, 80)
                sums_s[k] = sums_s[k] + jnp.where(kind == 0, front[k], mine) * mixed
                fronts[k, i] = front[k]
                front[k] = front[k] * decs[k] + mine
        for k in range(held):
            rate_d, res_d, decay_d, kind = local[k]
            dec, sum_r, sum_s, sum_m = decs[k], sums_r[k], sums_s[k], sums_m[k]
            is0, is1 = kind == 0, kind == 1

            def fold(x):
                x = jnp.sum(x, axis=0, keepdims=True)
                return x + shift(x, 64)

            raw_r = fold(sum_r)
            raw_s = fold(jnp.where(is0, sum_s + (positions * dec) * sum_m, 0.0)) + shift(
                fold(jnp.where(is1, sum_s, 0.0)), 112
            )
            lag = jnp.sum(recv1[:, k, 8:9, :], axis=0)
            weighted = jnp.where(
                sub == 0, lag, jnp.where(sub == 1, lag * (positions - 1 - lane).astype(F32), 0.0)
            )
            shared = lax.dot_general(
                weighted, decay_d, NN, precision=lax.Precision.HIGHEST, preferred_element_type=F32
            )
            raw_r = jnp.where(is0[0:1], raw_r, 0.0)
            raw_s = jnp.where(is0[0:1], raw_s, 0.0)
            raw_r = raw_r + shift(raw_r, 32)
            raw_s = raw_s + shift(raw_s, 32)
            raw_r = raw_r + shift(raw_r, 16) + shared[0:1]
            raw_s = (raw_s + shift(raw_s, 16) + shared[1:2]) * res_d * (-inv)
            grad1[k] = jnp.where(block[0:1] % 2 == 0, raw_r, raw_s)
        slot = ((my_d * n_x + my_x) * n_mid + my_z - mids[0]) * held
        for where in second_set:
            send(grad1, gather1.at[pl.ds(slot, held)], where, 2)
        gather1[pl.ds(slot, held)] = grad1[...]
        for k in range(held):
            _, res_d, _, kind = local[k]
            outer = (kind == 0) | (kind == 3)
            for i in range(n_ctx):
                both = jnp.where(kind == 0, shift(hold[k, i], 80), shift(fronts[k, i], 48)) * res_d
                low = shift(pltpu.roll(both, 4, 0), 32)
                msg2[i, k] = jnp.where(outer, both, low)[0:4]
        for peer in line:
            send(msg2.at[peer], recv2.at[my_owner], {"ctx": peer}, 1)
        recv2[my_owner] = msg2[me]

    n_second = n_side * n_mid

    @pl.when(own)
    def _():
        settle(recv_sem.at[2], gather1, (n_second - 1) * held)

    @pl.when(jnp.logical_not(own))
    def _():
        settle(recv_sem.at[2], gather1, n_second * held)

    quarter = lax.broadcasted_iota(jnp.int32, (n_z, TILE), 1) // 32
    pack = jnp.zeros((n_z, TILE), F32)
    for x in range(n_x):
        both = gather1[x * n_z : (x + 1) * n_z, 0, :]
        for d in range(1, n_dp):
            at = (d * n_x + x) * n_z
            both = both + gather1[at : at + n_z, 0, :]
        pack = jnp.where(quarter == x, both, pack)
    grad2[...] = pack
    my_third = my_c * n_y + my_y
    for where in third_set:
        send(grad2, gather2.at[my_third], where, 3)
    gather2[my_third] = pack
    by_role(recv_sem.at[1], recv2, n_owner - 1, n_owner)

    def finish(j, carry):
        heads = []
        tails = []
        for g in range(PER_TILE):
            at = j * PER_TILE + g
            top = recv2[at // held, at % held]
            m = jnp.concatenate([top, shift(top, 96)], axis=0)
            turned = shift(m, 64)
            for part in (m, turned):
                tails.append(jnp.where(block == g, part, 0.0))
                heads.append(jnp.where(block == (g + 3) % 8, part, 0.0))
        h_hi, h_lo = split(jnp.concatenate(heads, axis=0))
        b_hi, b_lo = split(jnp.concatenate(tails, axis=0))
        q_hi, q_lo, p_hi, p_lo = [tables[j, k] for k in range(4)]
        conv = convs[0, j] + (
            dot(h_hi, p_hi, NT) + (dot(h_lo, p_hi, NT) + dot(h_hi, p_lo, NT))
        )
        conv_grad = convs[1, j] + (
            dot(b_hi, q_hi, NT) + (dot(b_lo, q_hi, NT) + dot(b_hi, q_lo, NT))
        )
        conv = conv.astype(BF).T.astype(F32)
        conv_grad = conv_grad.astype(BF).T.astype(F32)
        vout[0, :, j * TILE : (j + 1) * TILE] = (vin[2, :, j * TILE : (j + 1) * TILE].astype(F32) * conv).astype(BF)
        vout[1, :, j * TILE : (j + 1) * TILE] = (conv_grad * vin[1, :, j * TILE : (j + 1) * TILE].astype(F32)).astype(BF)
        vout[2, :, j * TILE : (j + 1) * TILE] = (vin[3, :, j * TILE : (j + 1) * TILE].astype(F32) * conv).astype(BF)
        vout[3, :, j * TILE : (j + 1) * TILE] = (conv_grad * vin[0, :, j * TILE : (j + 1) * TILE].astype(F32)).astype(BF)
        return carry

    for j in range(tiles):
        finish(j, 0)

    settle(recv_sem.at[3], gather2, len(third_set))
    every = jnp.concatenate([gather2[i] for i in range(n_y * n_core)], axis=0)
    total = jnp.sum(jnp.sum(every * every, axis=0, keepdims=True), axis=1, keepdims=True)
    factor = CLIP / jnp.maximum(jnp.sqrt(total), CLIP)
    turned = every.T
    span = n_y * n_core * n_z
    for x in range(n_x):
        for k in range(2):
            at = x * 32 + k * ORD
            gout[k, :, x * span : (x + 1) * span] = turned[at : at + ORD] * factor
    by_role(send_sem.at[0], recv1, n_owner - 1, n_owner)

    @pl.when(own)
    def _():
        settle(send_sem.at[1], msg2, n_ctx - 1)
        settle(send_sem.at[2], gather1, len(second_set) * held)

    settle(send_sem.at[3], gather2, len(third_set))


def write_out(wide, small, out_conv, out_left, out_right, out_values, out_res, out_rate, sem):
    copies = [
        pltpu.make_async_copy(src, ref, sem)
        for src, ref in (
            (small.at[0], out_res),
            (small.at[1], out_rate),
            (wide.at[0], out_conv),
            (wide.at[1], out_left),
            (wide.at[2], out_right),
            (wide.at[3], out_values),
        )
    ]
    for copy in copies:
        copy.start()
    pltpu.make_async_copy(wide, wide, sem).wait()
    pltpu.make_async_copy(small, small, sem).wait()


def solution(mesh):
    n_ctx, n_tensor, n_dp = mesh.shape["ctx"], mesh.shape["tensor"], mesh.shape["dp"]

    def on_device(left_gate, right_gate, values, grad_out, residues, decay_rates):
        positions, channels = left_gate.shape[1:]
        tiles = channels // TILE
        groups = channels // GSIZE
        held = groups // (n_ctx // N_Z * (N_Z - 2))
        flat = [x.reshape(positions, channels) for x in (left_gate, right_gate, values, grad_out)]
        wide = jax.ShapeDtypeStruct((positions, channels), BF)
        small = jax.ShapeDtypeStruct(residues.shape[::-1], F32)
        in_hbm = pl.BlockSpec(memory_space=pltpu.HBM)
        in_vmem = pl.BlockSpec(memory_space=pltpu.VMEM)
        outs = pl.pallas_call(
            functools.partial(kernel, n_ctx, N_Z, n_tensor, N_CORE, n_dp),
            out_shape=(
                jax.ShapeDtypeStruct((4, positions, channels), BF),
                jax.ShapeDtypeStruct((2,) + residues.shape[::-1], F32),
            ),
            in_specs=[in_hbm] * 6,
            out_specs=(in_vmem, in_vmem),
            scratch_shapes=[
                pltpu.VMEM((4, positions, channels), BF),
                pltpu.VMEM((2,) + residues.shape, F32),
                pltpu.VMEM((4, tiles, TILE, TILE), BF),
                pltpu.VMEM((tiles, 6, positions, TILE), BF),
                pltpu.VMEM((tiles, PER_TILE, positions), F32),
                pltpu.VMEM((2, tiles, TILE, positions), F32),
                pltpu.VMEM((groups, 9, TILE), F32),
                pltpu.VMEM((n_ctx, held, 9, TILE), F32),
                pltpu.VMEM((held, n_ctx, 8, TILE), F32),
                pltpu.VMEM((held, n_ctx, 8, TILE), F32),
                pltpu.VMEM((n_ctx, held, 4, TILE), F32),
                pltpu.VMEM((groups // held, held, 4, TILE), F32),
                pltpu.VMEM((held, 1, TILE), F32),
                pltpu.VMEM((n_dp * n_tensor // N_CORE * N_Z * held, 1, TILE), F32),
                pltpu.VMEM((N_Z, TILE), F32),
                pltpu.VMEM((n_ctx // N_Z * N_CORE, N_Z, TILE), F32),
                pltpu.SemaphoreType.DMA,
                pltpu.SemaphoreType.DMA,
                pltpu.SemaphoreType.DMA((4,)),
                pltpu.SemaphoreType.DMA((4,)),
            ],
            compiler_params=pltpu.CompilerParams(
                collective_id=0, has_side_effects=True, vmem_limit_bytes=16 * 1024 * 1024
            ),
        )(*[pltpu.with_memory_space_constraint(x, pltpu.HBM) for x in (*flat, residues.T, decay_rates.T)])
        outs = pl.pallas_call(
            write_out,
            out_shape=(wide, wide, wide, wide, small, small),
            in_specs=[pl.BlockSpec(memory_space=pl.ANY)] * 2,
            out_specs=(in_hbm,) * 6,
            scratch_shapes=[pltpu.SemaphoreType.DMA],
            compiler_params=pltpu.CompilerParams(vmem_limit_bytes=1024 * 1024),
        )(*outs)
        full = [x.reshape(1, positions, channels) for x in outs[:4]]
        return (*full, outs[4].T, outs[5].T)

    wide = P("dp", "ctx", "tensor")
    return jax.shard_map(
        on_device,
        mesh=mesh,
        in_specs=(wide, wide, wide, wide, P(), P()),
        out_specs=(wide, wide, wide, wide, P(), P()),
        check_vma=False,
    )
```

```python
import functools

import jax
import jax.numpy as jnp
from jax import lax
from jax.experimental import pallas as pl
from jax.experimental.pallas import tpu as pltpu
from jax.sharding import PartitionSpec as P

MESH = pl.DeviceIdType.MESH
BF = jnp.bfloat16
F32 = jnp.float32
GSIZE = 16
ORD = 16
TILE = 128
PER_TILE = TILE // GSIZE
CLIP = 32.0
N_Z = 4
N_CORE = 2
NT = (((1,), (1,)), ((), ()))
NN = (((1,), (0,)), ((), ()))


def dot(a, b, dims=NN):
    return lax.dot_general(a, b, dims, preferred_element_type=F32)


def split(x):
    hi = x.astype(BF)
    return hi, (x - hi.astype(F32)).astype(BF)


def lanes8(x):
    return jnp.concatenate([x] * PER_TILE, axis=1)


def shift(x, amount):
    amount = amount % TILE
    return x if amount == 0 else pltpu.roll(x, amount, 1)


def decays(rate, positions, top=None):
    sub = lax.broadcasted_iota(jnp.int32, (8, TILE), 0).astype(F32)
    blocks = positions // 8
    step = jnp.exp(-8.0 * rate)
    now = jnp.exp(-rate * (sub if top is None else top - (positions - 8) - sub))
    rows = [now]
    for _ in range(blocks - 1):
        now = now * step
        rows.append(now)
    if top is not None:
        rows = rows[::-1]
    return jnp.concatenate(rows, axis=0)


def kernel(
    n_ctx,
    n_z,
    n_tensor,
    n_core,
    n_dp,
    left_hbm,
    right_hbm,
    values_hbm,
    grad_hbm,
    res_hbm,
    rate_hbm,
    vout,
    gout,
    vin,
    par,
    gst,
    tables,
    taps,
    convs,
    msg1,
    recv1,
    hold,
    fronts,
    msg2,
    recv2,
    grad1,
    gather1,
    grad2,
    gather2,
    in_sem,
    par_sem,
    send_sem,
    recv_sem,
):
    me = lax.axis_index("ctx")
    my_t = lax.axis_index("tensor")
    my_d = lax.axis_index("dp")
    positions = vin.shape[1]
    tiles = vin.shape[2] // TILE
    seq = n_ctx * positions
    groups = tiles * PER_TILE
    inv = 1.0 / seq

    my_y, my_z = me // n_z, lax.rem(me, n_z)
    my_x, my_c = my_t // n_core, lax.rem(my_t, n_core)
    n_y, n_x = n_ctx // n_z, n_tensor // n_core
    ring = sorted(range(n_y), key=lambda o: -min(o, n_y - o))
    line = [
        (lax.rem(my_y + dy, n_y) * n_z + lax.rem(my_z + dz, n_z))
        for dy in ring
        for dz in reversed(range(n_z))
        if dy or dz
    ]
    mids = tuple(range(1, n_z - 1))
    n_mid = len(mids)
    own = (my_z >= mids[0]) & (my_z <= mids[-1])
    held = groups // (n_y * n_mid)
    my_owner = my_y * n_mid + my_z - mids[0]

    def owner(dy, m):
        y = lax.rem(my_y + dy, n_y)
        return y * n_mid + m - mids[0], y * n_z + m

    owners = [owner(dy, m) for dy in ring if dy for m in mids]
    near = [owner(0, m) for m in mids]

    def spread(dd, dx, z):
        d, x = lax.rem(my_d + dd, n_dp), lax.rem(my_x + dx, n_x)
        return {"dp": d, "tensor": x * n_core + my_c, "ctx": my_y * n_z + z}

    turns = [
        (dd, dx)
        for dd in reversed(range(n_dp))
        for dx in sorted(range(n_x), key=lambda o: -min(o, n_x - o))
    ]
    second_set = [
        spread(dd, dx, lax.rem(my_z + dz, n_z))
        for dd, dx in turns
        for dz in reversed(range(n_z))
        if dd or dx or dz
    ]

    def across(dy, dc):
        y, c = lax.rem(my_y + dy, n_y), lax.rem(my_c + dc, n_core)
        return c * n_y + y, {"tensor": my_x * n_core + c, "ctx": y * n_z + my_z}

    third_set = [across(dy, dc)[1] for dy in ring for dc in reversed(range(n_core)) if dy or dc]

    barrier = pltpu.get_barrier_semaphore()

    def greet(where):
        pl.semaphore_signal(barrier, inc=1, device_id=where, device_id_type=MESH)

    ends = (0, n_z - 1)

    @pl.when(own)
    def _():
        for dy in ring:
            for z in ends:
                greet({"ctx": lax.rem(my_y + dy, n_y) * n_z + z})
        for dd, dx in turns:
            if dd or dx:
                for z in ends:
                    greet(spread(dd, dx, z))
        greet({"ctx": my_y * n_z + mids[0] + mids[-1] - my_z})

    for _, peer in owners:
        greet({"ctx": peer})
    for dd, dx in turns:
        if dd or dx:
            for z in mids:
                greet(spread(dd, dx, z))
    for dy in ring:
        for dc in range(1, n_core):
            greet(across(dy, dc)[1])

    @pl.when(jnp.logical_not(own))
    def _():
        for dy in ring:
            if dy:
                greet(across(dy, 0)[1])
        for _, peer in near:
            greet({"ctx": peer})

    n_side = n_dp * n_x
    met_own = n_ctx - 1 + (n_side - 1) * n_z + n_y * (n_core - 1)
    met_end = n_y * n_mid + (n_side - 1) * n_mid + n_y * n_core - 1
    met = jnp.where(own, met_own, met_end)

    for k, ref in enumerate((res_hbm, rate_hbm)):
        pltpu.make_async_copy(ref, gout.at[k], par_sem).start()
    for a, ref in enumerate((left_hbm, values_hbm, right_hbm, grad_hbm)):
        pltpu.make_async_copy(ref, vin.at[a], in_sem).start()
    pltpu.make_async_copy(gout, gout, par_sem).wait()
    for k in range(2):
        par[k] = gout[k].T
    first = pl.multiple_of(my_t * groups, groups)

    lane = lax.broadcasted_iota(jnp.int32, (8, TILE), 1)
    sub = lax.broadcasted_iota(jnp.int32, (8, TILE), 0)
    block = lane // GSIZE
    row_i = lax.broadcasted_iota(jnp.int32, (TILE, TILE), 0)
    col_i = lax.broadcasted_iota(jnp.int32, (TILE, TILE), 1)
    pos_col = row_i.astype(F32)

    slopes = []
    for j in range(tiles):
        pick = pl.ds(pl.multiple_of(first + j * PER_TILE, PER_TILE), PER_TILE)
        rates = jnp.where(block == sub, lanes8(par[1, pick, :]), 0.0)
        resid = jnp.where(block == sub, lanes8(par[0, pick, :]), 0.0)
        rate = jnp.sum(rates, axis=0, keepdims=True) * inv
        ahead = decays(rate, positions, positions)
        ahead1 = decays(shift(rate, 16), positions, positions) * (positions - pos_col)
        after2 = decays(shift(rate, 32), positions) * pos_col
        after = decays(shift(rate, 48), positions)
        q_hi, q_lo = split(ahead)
        p_hi, p_lo = split(after)
        tables[j, 0] = q_hi
        tables[j, 1] = q_lo
        tables[j, 2] = p_hi
        tables[j, 3] = p_lo
        tables[j, 4] = ahead1.astype(BF)
        tables[j, 5] = after2.astype(BF)
        r_hi, r_lo = split(shift(resid, 48))
        taps[j] = dot(r_hi, p_hi, NT) + (dot(r_lo, p_hi, NT) + dot(r_hi, p_lo, NT))

    pltpu.make_async_copy(vin, vin, in_sem).wait()
    mirror = row_i + col_i
    flip = jnp.where(mirror == positions - 1, 1.0, 0.0).astype(BF)
    for j in range(tiles):
        gated = (vin[0, :, j * TILE : (j + 1) * TILE].astype(F32) * vin[1, :, j * TILE : (j + 1) * TILE].astype(F32)).astype(BF)
        signal = (vin[2, :, j * TILE : (j + 1) * TILE].astype(F32) * vin[3, :, j * TILE : (j + 1) * TILE].astype(F32)).astype(BF)
        gst[0, j] = gated
        gst[1, j] = dot(flip, signal).astype(BF)
        gated_t = gated.T
        signal_t = signal.T
        gst[2, j] = gated_t
        gst[3, j] = signal_t
        kinds = (
            dot(gated_t, tables[j, 0]) + dot(gated_t, tables[j, 1]),
            dot(gated_t, tables[j, 4]),
            dot(signal_t, tables[j, 5]),
            dot(signal_t, tables[j, 2]) + dot(signal_t, tables[j, 3]),
        )
        for g in range(PER_TILE):
            which = (block - g) & 7
            halves = []
            for half in range(2):
                at = g * GSIZE + 8 * half
                part = kinds[3][at : at + 8]
                for k in (2, 1, 0):
                    part = jnp.where(which == k, kinds[k][at : at + 8], part)
                halves.append(part)
            msg1[j * PER_TILE + g, 0:8, :] = jnp.where(
                which < 4, halves[0], shift(halves[1], 64)
            )

    for j in range(tiles):
        gated = gst[0, j]
        flipped = gst[1, j]
        for g in range(PER_TILE):
            only = jnp.where(col_i // GSIZE == g, gated.astype(F32), 0.0).astype(BF)
            pair = jnp.where(mirror < positions, dot(only, flipped, NT), 0.0)
            skew = pltpu.roll(pair, 0, 1, stride=1, stride_axis=0)
            msg1[j * PER_TILE + g, 8:9, :] = jnp.sum(skew, axis=0, keepdims=True)

    def send(src, dst, where, k):
        pltpu.make_async_remote_copy(
            src_ref=src,
            dst_ref=dst,
            send_sem=send_sem.at[k],
            recv_sem=recv_sem.at[k],
            device_id=where,
            device_id_type=MESH,
        ).start()

    def settle(sem, dst, count):
        part = dst.at[pl.ds(0, count)]
        pltpu.make_async_copy(part, part, sem).wait()

    def by_role(sem, dst, count_own, count_end):
        @pl.when(own)
        def _():
            settle(sem, dst, count_own)

        @pl.when(jnp.logical_not(own))
        def _():
            settle(sem, dst, count_end)

    n_owner = n_y * n_mid

    pl.semaphore_wait(barrier, met)
    for o, peer in owners:
        send(msg1.at[pl.ds(held * o, held)], recv1.at[me], {"ctx": peer}, 0)
    for o, peer in near:

        @pl.when(peer != me)
        def _():
            send(msg1.at[pl.ds(held * o, held)], recv1.at[me], {"ctx": peer}, 0)

    later = col_i >= row_i

    def inside(j, carry):
        rows = taps[j].astype(BF).astype(F32)
        for g in range(PER_TILE):
            wide = jnp.broadcast_to(rows[g : g + 1], (TILE, TILE))
            turned = pltpu.roll(wide, 0, 1, stride=1, stride_axis=0)
            upper = jnp.where(later, turned, 0.0).astype(BF)
            at = g * GSIZE
            convs[0, j, at : at + GSIZE, :] = dot(gst[2, j, at : at + GSIZE, :], upper)
            convs[1, j, at : at + GSIZE, :] = dot(gst[3, j, at : at + GSIZE, :], upper, NT)
        return carry

    lax.fori_loop(0, tiles, inside, 0)

    @pl.when(own)
    def _():
        recv1[me] = msg1[pl.ds(held * my_owner, held)]
        local = []
        for k in range(held):
            at = held * my_owner + k
            rate_d = lanes8(par[1, pl.ds(first + at, 1), :]) * inv
            res_d = lanes8(par[0, pl.ds(first + at, 1), :])
            decay_d = decays(rate_d, positions, positions - 1)
            local.append((rate_d, res_d, decay_d, (block - at) & 3))
        settle(recv_sem.at[0], recv1, n_ctx - 1)
        zero = jnp.zeros((8, TILE), F32)
        decs = [jnp.exp(-local[k][0] * positions) for k in range(held)]
        back = [zero] * held
        for i in reversed(range(n_ctx)):
            for k in range(held):
                hold[k, i] = back[k]
                back[k] = back[k] * decs[k] + recv1[i, k, 0:8, :]
        front, sums_r, sums_s, sums_m = [zero] * held, [zero] * held, [zero] * held, [zero] * held
        for i in range(n_ctx):
            for k in range(held):
                kind = local[k][3]
                mine = recv1[i, k, 0:8, :]
                behind = hold[k, i]
                mixed = shift(jnp.where(kind == 2, mine, behind), 96)
                sums_r[k] = sums_r[k] + front[k] * shift(mine, 80)
                sums_m[k] = sums_m[k] + front[k] * shift(behind, 80)
                sums_s[k] = sums_s[k] + jnp.where(kind == 0, front[k], mine) * mixed
                fronts[k, i] = front[k]
                front[k] = front[k] * decs[k] + mine
        for k in range(held):
            rate_d, res_d, decay_d, kind = local[k]
            dec, sum_r, sum_s, sum_m = decs[k], sums_r[k], sums_s[k], sums_m[k]
            is0, is1 = kind == 0, kind == 1

            def fold(x):
                x = jnp.sum(x, axis=0, keepdims=True)
                return x + shift(x, 64)

            raw_r = fold(sum_r)
            raw_s = fold(jnp.where(is0, sum_s + (positions * dec) * sum_m, 0.0)) + shift(
                fold(jnp.where(is1, sum_s, 0.0)), 112
            )
            lag = jnp.sum(recv1[:, k, 8:9, :], axis=0)
            weighted = jnp.where(
                sub == 0, lag, jnp.where(sub == 1, lag * (positions - 1 - lane).astype(F32), 0.0)
            )
            shared = lax.dot_general(
                weighted, decay_d, NN, precision=lax.Precision.HIGHEST, preferred_element_type=F32
            )
            raw_r = jnp.where(is0[0:1], raw_r, 0.0)
            raw_s = jnp.where(is0[0:1], raw_s, 0.0)
            raw_r = raw_r + shift(raw_r, 32)
            raw_s = raw_s + shift(raw_s, 32)
            raw_r = raw_r + shift(raw_r, 16) + shared[0:1]
            raw_s = (raw_s + shift(raw_s, 16) + shared[1:2]) * res_d * (-inv)
            grad1[k] = jnp.where(block[0:1] % 2 == 0, raw_r, raw_s)
        slot = ((my_d * n_x + my_x) * n_mid + my_z - mids[0]) * held
        for where in second_set:
            send(grad1, gather1.at[pl.ds(slot, held)], where, 2)
        gather1[pl.ds(slot, held)] = grad1[...]
        for k in range(held):
            _, res_d, _, kind = local[k]
            outer = (kind == 0) | (kind == 3)
            for i in range(n_ctx):
                both = jnp.where(kind == 0, shift(hold[k, i], 80), shift(fronts[k, i], 48)) * res_d
                low = shift(pltpu.roll(both, 4, 0), 32)
                msg2[i, k] = jnp.where(outer, both, low)[0:4]
        for peer in line:
            send(msg2.at[peer], recv2.at[my_owner], {"ctx": peer}, 1)
        recv2[my_owner] = msg2[me]

    n_second = n_side * n_mid

    @pl.when(own)
    def _():
        settle(recv_sem.at[2], gather1, (n_second - 1) * held)

    @pl.when(jnp.logical_not(own))
    def _():
        settle(recv_sem.at[2], gather1, n_second * held)

    quarter = lax.broadcasted_iota(jnp.int32, (n_z, TILE), 1) // 32
    pack = jnp.zeros((n_z, TILE), F32)
    for x in range(n_x):
        both = gather1[x * n_z : (x + 1) * n_z, 0, :]
        for d in range(1, n_dp):
            at = (d * n_x + x) * n_z
            both = both + gather1[at : at + n_z, 0, :]
        pack = jnp.where(quarter == x, both, pack)
    grad2[...] = pack
    my_third = my_c * n_y + my_y
    for where in third_set:
        send(grad2, gather2.at[my_third], where, 3)
    gather2[my_third] = pack
    by_role(recv_sem.at[1], recv2, n_owner - 1, n_owner)

    def finish(j, carry):
        heads = []
        tails = []
        for g in range(PER_TILE):
            at = j * PER_TILE + g
            top = recv2[at // held, at % held]
            m = jnp.concatenate([top, shift(top, 96)], axis=0)
            turned = shift(m, 64)
            for part in (m, turned):
                tails.append(jnp.where(block == g, part, 0.0))
                heads.append(jnp.where(block == (g + 3) % 8, part, 0.0))
        h_hi, h_lo = split(jnp.concatenate(heads, axis=0))
        b_hi, b_lo = split(jnp.concatenate(tails, axis=0))
        q_hi, q_lo, p_hi, p_lo = [tables[j, k] for k in range(4)]
        conv = convs[0, j] + (
            dot(h_hi, p_hi, NT) + (dot(h_lo, p_hi, NT) + dot(h_hi, p_lo, NT))
        )
        conv_grad = convs[1, j] + (
            dot(b_hi, q_hi, NT) + (dot(b_lo, q_hi, NT) + dot(b_hi, q_lo, NT))
        )
        conv = conv.astype(BF).T.astype(F32)
        conv_grad = conv_grad.astype(BF).T.astype(F32)
        vout[0, :, j * TILE : (j + 1) * TILE] = (vin[2, :, j * TILE : (j + 1) * TILE].astype(F32) * conv).astype(BF)
        vout[1, :, j * TILE : (j + 1) * TILE] = (conv_grad * vin[1, :, j * TILE : (j + 1) * TILE].astype(F32)).astype(BF)
        vout[2, :, j * TILE : (j + 1) * TILE] = (vin[3, :, j * TILE : (j + 1) * TILE].astype(F32) * conv).astype(BF)
        vout[3, :, j * TILE : (j + 1) * TILE] = (conv_grad * vin[0, :, j * TILE : (j + 1) * TILE].astype(F32)).astype(BF)
        return carry

    for j in range(tiles):
        finish(j, 0)

    by_role(send_sem.at[0], recv1, n_owner - 1, n_owner)

    @pl.when(own)
    def _():
        settle(send_sem.at[1], msg2, n_ctx - 1)
        settle(send_sem.at[2], gather1, len(second_set) * held)

    settle(recv_sem.at[3], gather2, len(third_set))
    every = jnp.concatenate([gather2[i] for i in range(n_y * n_core)], axis=0)
    total = jnp.sum(jnp.sum(every * every, axis=0, keepdims=True), axis=1, keepdims=True)
    factor = CLIP / jnp.maximum(jnp.sqrt(total), CLIP)
    turned = every.T
    span = n_y * n_core * n_z
    for x in range(n_x):
        for k in range(2):
            at = x * 32 + k * ORD
            gout[k, :, x * span : (x + 1) * span] = turned[at : at + ORD] * factor
    settle(send_sem.at[3], gather2, len(third_set))


def write_out(wide, small, out_conv, out_left, out_right, out_values, out_res, out_rate, sem):
    copies = [
        pltpu.make_async_copy(src, ref, sem)
        for src, ref in (
            (small.at[0], out_res),
            (small.at[1], out_rate),
            (wide.at[0], out_conv),
            (wide.at[1], out_left),
            (wide.at[2], out_right),
            (wide.at[3], out_values),
        )
    ]
    for copy in copies:
        copy.start()
    pltpu.make_async_copy(wide, wide, sem).wait()
    pltpu.make_async_copy(small, small, sem).wait()


def solution(mesh):
    n_ctx, n_tensor, n_dp = mesh.shape["ctx"], mesh.shape["tensor"], mesh.shape["dp"]

    def on_device(left_gate, right_gate, values, grad_out, residues, decay_rates):
        positions, channels = left_gate.shape[1:]
        tiles = channels // TILE
        groups = channels // GSIZE
        held = groups // (n_ctx // N_Z * (N_Z - 2))
        flat = [x.reshape(positions, channels) for x in (left_gate, right_gate, values, grad_out)]
        wide = jax.ShapeDtypeStruct((positions, channels), BF)
        small = jax.ShapeDtypeStruct(residues.shape[::-1], F32)
        in_hbm = pl.BlockSpec(memory_space=pltpu.HBM)
        in_vmem = pl.BlockSpec(memory_space=pltpu.VMEM)
        outs = pl.pallas_call(
            functools.partial(kernel, n_ctx, N_Z, n_tensor, N_CORE, n_dp),
            out_shape=(
                jax.ShapeDtypeStruct((4, positions, channels), BF),
                jax.ShapeDtypeStruct((2,) + residues.shape[::-1], F32),
            ),
            in_specs=[in_hbm] * 6,
            out_specs=(in_vmem, in_vmem),
            scratch_shapes=[
                pltpu.VMEM((4, positions, channels), BF),
                pltpu.VMEM((2,) + residues.shape, F32),
                pltpu.VMEM((4, tiles, TILE, TILE), BF),
                pltpu.VMEM((tiles, 6, positions, TILE), BF),
                pltpu.VMEM((tiles, PER_TILE, positions), F32),
                pltpu.VMEM((2, tiles, TILE, positions), F32),
                pltpu.VMEM((groups, 9, TILE), F32),
                pltpu.VMEM((n_ctx, held, 9, TILE), F32),
                pltpu.VMEM((held, n_ctx, 8, TILE), F32),
                pltpu.VMEM((held, n_ctx, 8, TILE), F32),
                pltpu.VMEM((n_ctx, held, 4, TILE), F32),
                pltpu.VMEM((groups // held, held, 4, TILE), F32),
                pltpu.VMEM((held, 1, TILE), F32),
                pltpu.VMEM((n_dp * n_tensor // N_CORE * N_Z * held, 1, TILE), F32),
                pltpu.VMEM((N_Z, TILE), F32),
                pltpu.VMEM((n_ctx // N_Z * N_CORE, N_Z, TILE), F32),
                pltpu.SemaphoreType.DMA,
                pltpu.SemaphoreType.DMA,
                pltpu.SemaphoreType.DMA((4,)),
                pltpu.SemaphoreType.DMA((4,)),
            ],
            compiler_params=pltpu.CompilerParams(
                collective_id=0, has_side_effects=True, vmem_limit_bytes=16 * 1024 * 1024
            ),
        )(*[pltpu.with_memory_space_constraint(x, pltpu.HBM) for x in (*flat, residues.T, decay_rates.T)])
        outs = pl.pallas_call(
            write_out,
            out_shape=(wide, wide, wide, wide, small, small),
            in_specs=[pl.BlockSpec(memory_space=pl.ANY)] * 2,
            out_specs=(in_hbm,) * 6,
            scratch_shapes=[pltpu.SemaphoreType.DMA],
            compiler_params=pltpu.CompilerParams(vmem_limit_bytes=1024 * 1024),
        )(*outs)
        full = [x.reshape(1, positions, channels) for x in outs[:4]]
        return (*full, outs[4].T, outs[5].T)

    wide = P("dp", "ctx", "tensor")
    return jax.shard_map(
        on_device,
        mesh=mesh,
        in_specs=(wide, wide, wide, wide, P(), P()),
        out_specs=(wide, wide, wide, wide, P(), P()),
        check_vma=False,
    )
```
